32 devices in a mesh: comp: 16 (over z, x, core), space: 2 (over y).
Axes of the slice: x: 2, y: 2, z: 4, core: 2. Of those that a mesh axis runs over, the one named last changes fastest.
Arguments:
- spectrum: float32 [1152, 16384], P(None, ('comp', 'space')), may hold values from 0.05 to 1
- wind_field: float32 [2, 16384], P(None, ('comp', 'space')), may hold values from -4 to 4
- coupling: bfloat16 [1152, 1152], replicated, may hold values from -0.1875 to 0.1875
- growth: float32 [32], replicated, may hold values from 0.02 to 0.2
- dissipation: float32 [32], replicated, may hold values from 0.1 to 1
- group_speed: float32 [32, 32], replicated, may hold values from 0.1 to 0.45
- refraction: float32 [32, 32], replicated, may hold values from -0.5 to 0.5
- depths: float32 [32], replicated, may hold values from 0.1 to 1
- sea_mask: int32 [128, 128], P('space'), may hold values 0 or 1
- depth_index: int32 [128, 128], P('space'), may hold values from 0 to 31
Outputs:
- spectrum_out: float32 [1152, 16384], P(None, ('comp', 'space'))
The draws below stay inside these ranges and needn't reach their ends.
All inputs are finite; a program needn't handle non-finite values. No bound on the sum of `sea_mask` on one device may be relied on, other than what follows from the above.
Results may differ from the reference program's by a relative error of at most 0.00051.
Values sent between devices are 32-bit elements; how exact they have to be, the bound alone decides.
No kernel may reach another device: no remote copies, remote signals or barrier semaphores. Data moves between devices by JAX's collectives and lax.ppermute only.
A program may use at most 64 MiB of HBM per device.

```python
import math
import jax
import jax.numpy as jnp
from jax import lax

NF = 32
ND = 36
K = 1152
NDEP = 32
RB = 4
NY = 128
SUBSTEPS = 3
NX = 128
POINTS = 16384
N_COMP = 16
N_SPACE = 2


def with_ends(result, own_key, least, largest):
    dims = result.shape
    place = [jax.random.randint(jax.random.fold_in(own_key, axis), (), 0, dims[axis]) for axis in range(len(dims))]
    result = result.at[tuple(place)].set(least)
    longest = dims.index(max(dims))
    place[longest] = (place[longest] + 1) % dims[longest]
    return result.at[tuple(place)].set(largest)


def steps_of(rng, dims, pieces, smallest, top_value):
    def one(axis_at, parts):
        steps = jax.random.uniform(jax.random.fold_in(jax.random.fold_in(rng, 6), axis_at), (parts,), jnp.float32, smallest / len(pieces), top_value / len(pieces))
        return jnp.repeat(jnp.exp(steps), dims[axis_at] // parts).reshape((-1,) + (1,) * (len(dims) - axis_at - 1))

    loudness = one(*pieces[0])
    for cut in pieces[1:]:
        loudness = loudness * one(*cut)
    return loudness


def normal_values(stream_key, dims, scale, most, split=(), held_as=jnp.bfloat16):
    loudness = steps_of(stream_key, dims, split, -0.22, 0.18) if split else 1.0
    result = jax.random.normal(stream_key, dims, jnp.float32) * scale * loudness
    return jnp.minimum(jnp.maximum(result, -most), most).astype(held_as)


def setup_inputs(seed: int = 0) -> dict:
    keys = jax.random.split(jax.random.key(seed), 11)
    spectrum = jnp.clip(jnp.exp(math.log(1.0) - 2.9957323 * jax.random.uniform(keys[0], (K, POINTS), jnp.float32) ** steps_of(keys[0], (K, POINTS), ((1, 32),), -0.2, 0.2)), 0.05, 1.0)
    wind_field = normal_values(keys[1], (2, POINTS), 1.0, 4.0, ((1, 32),), jnp.float32)
    coupling = normal_values(keys[2], (K, K), K ** -0.5, 0.1875)
    growth = jnp.clip(jnp.exp(jax.random.uniform(keys[3], (NF,), jnp.float32, math.log(0.02), math.log(0.2))), 0.02, 0.2)
    dissipation = jnp.clip(jnp.exp(jax.random.uniform(keys[4], (NF,), jnp.float32, math.log(0.1), math.log(1.0))), 0.1, 1.0)
    group_speed = jnp.clip(jnp.exp(jax.random.uniform(keys[5], (NF, NDEP), jnp.float32, math.log(0.1), math.log(0.45))), 0.1, 0.45)
    refraction = jnp.clip(jax.random.uniform(keys[6], (NF, NDEP), jnp.float32, -0.5, 0.5), -0.5, 0.5)
    depths = jnp.clip(jax.random.uniform(keys[7], (NDEP,), jnp.float32, 0.1, 1.0), 0.1, 1.0)
    sea_mask = with_ends((jax.random.randint(keys[8], (NX, NY), 0, 10) < 9).astype(jnp.int32), jax.random.fold_in(keys[8], 1), 0, 1)
    depth_index = with_ends(jax.random.randint(keys[9], (NX, NY), 0, NDEP), jax.random.fold_in(keys[9], 1), 0, NDEP - 1).astype(jnp.int32)
    return {"spectrum": spectrum, "wind_field": wind_field, "coupling": coupling, "growth": growth, "dissipation": dissipation, "group_speed": group_speed, "refraction": refraction, "depths": depths, "sea_mask": sea_mask, "depth_index": depth_index}


def direction_angles():
    return 2.0 * jnp.pi * jnp.arange(ND, dtype=jnp.float32) / ND


def source_terms(energy, wind_block, coupling, growth, dissipation):
    nfreq = growth.shape[0]
    angles = direction_angles()
    projected = jnp.cos(angles)[:, None] * wind_block[0][None, :] + jnp.sin(angles)[:, None] * wind_block[1][None, :]
    forcing = jnp.maximum(projected, 0.0)
    driving = growth[:, None, None] * (forcing * forcing)[None]
    average = jnp.mean(energy, axis=0)
    damping = dissipation[:, None, None] * (average / (average + 1.0))[None, None, :]
    nonlinear = jnp.dot(coupling, energy.astype(jnp.bfloat16), preferred_element_type=jnp.float32)
    shaped = energy.reshape(nfreq, ND, -1)
    return (shaped + (driving - damping) * shaped).reshape(energy.shape) + 0.25 * nonlinear


def face_flux(behind, centre, forward, beyond, courant):
    central = 0.5 * (centre + forward) - 0.5 * courant * (forward - centre)
    curvature = jnp.where(courant >= 0.0, forward - 2.0 * centre + behind, beyond - 2.0 * forward + centre)
    return courant * (central - (1.0 - courant * courant) / 6.0 * curvature)


def cut_along(values, offset, length, along):
    return lax.slice_in_dim(values, offset, offset + length, axis=along)


def advect(padded, speeds, weight, along):
    inner_count = padded.shape[along] - 4
    courant = 0.5 * (cut_along(speeds, 1, inner_count + 1, along) + cut_along(speeds, 2, inner_count + 1, along))
    if weight is not None:
        courant = courant * cut_along(weight, 1, inner_count + 1, along) * cut_along(weight, 2, inner_count + 1, along)
    face_values = face_flux(cut_along(padded, 0, inner_count + 1, along), cut_along(padded, 1, inner_count + 1, along),
                            cut_along(padded, 2, inner_count + 1, along), cut_along(padded, 3, inner_count + 1, along), courant)
    return cut_along(padded, 2, inner_count, along) - (cut_along(face_values, 1, inner_count, along) - cut_along(face_values, 0, inner_count, along))


def pad_zero(values, along, width):
    padding = [(0, 0)] * values.ndim
    padding[along] = (width, width)
    return jnp.pad(values, padding)


def wrap_dirs(values, along):
    length = values.shape[along]
    return jnp.concatenate([cut_along(values, length - 2, 2, along), values, cut_along(values, 0, 2, along)], axis=along)


def surface_slopes(height):
    rows_padded = jnp.pad(height, ((1, 1), (0, 0)))
    cols_padded = jnp.pad(height, ((0, 0), (1, 1)))
    return 0.5 * (rows_padded[2:] - rows_padded[:-2]), 0.5 * (cols_padded[:, 2:] - cols_padded[:, :-2])


def transport_speeds(speed_pts, refract_pts, height):
    angles = direction_angles()
    cosine_dir = jnp.cos(angles)[:, None, None]
    sine_dir = jnp.sin(angles)[:, None, None]
    slope_x, slope_y = surface_slopes(height)
    speed_wide = jnp.expand_dims(speed_pts, -3)
    speed_x = speed_wide * cosine_dir
    speed_y = speed_wide * sine_dir
    speed_dir = jnp.expand_dims(refract_pts, -3) * (sine_dir * slope_x - cosine_dir * slope_y)
    return speed_x, speed_y, speed_dir


def cross_passes(energy, speed_y, speed_dir, mask_wide):
    y_axis = energy.ndim - 1
    dir_axis = energy.ndim - 3
    energy = advect(pad_zero(energy, y_axis, 2), pad_zero(speed_y, y_axis, 2), pad_zero(mask_wide, y_axis, 2), y_axis)
    energy = advect(wrap_dirs(energy, dir_axis), wrap_dirs(speed_dir, dir_axis), None, dir_axis)
    return energy * mask_wide


def reference(spectrum, wind_field, coupling, growth, dissipation, group_speed, refraction, depths, sea_mask, depth_index):
    block_count = N_COMP * N_SPACE
    block_points = RB * NY
    blocks = jnp.moveaxis(spectrum.reshape(K, block_count, block_points), 1, 0)
    wind_blocks = jnp.moveaxis(wind_field.reshape(2, block_count, block_points), 1, 0)
    sourced = lax.map(lambda paired: source_terms(paired[0], paired[1], coupling, growth, dissipation), (blocks, wind_blocks))
    grid_energy = sourced.reshape(N_COMP, N_SPACE, NF, ND, RB, NY).transpose(2, 3, 1, 0, 4, 5).reshape(NF, ND, NX, NY)
    mask_float = sea_mask.astype(jnp.float32)
    height = depths[depth_index] * mask_float
    mask_wide = mask_float[None]

    def one_freq(freq_item):
        energy, speed_row, refract_row = freq_item
        speed_x, speed_y, speed_dir = transport_speeds(speed_row[depth_index], refract_row[depth_index], height)
        for substep in range(SUBSTEPS):
            energy = advect(pad_zero(energy, 1, 2), pad_zero(speed_x, 1, 2), pad_zero(mask_wide, 1, 2), 1)
            energy = cross_passes(energy, speed_y, speed_dir, mask_wide)
        return energy

    moved = lax.map(one_freq, (grid_energy, group_speed, refraction))
    return moved.reshape(NF, ND, N_SPACE, N_COMP, RB, NY).transpose(0, 1, 3, 2, 4, 5).reshape(K, POINTS)
```

```python
import functools

import jax
import jax.numpy as jnp
import numpy as np
from jax import lax
from jax.experimental import pallas as pl
from jax.experimental.pallas import tpu as pltpu
from jax.sharding import PartitionSpec as P

ND = 36
LANES = 128
TILE = 8
CHUNKS = 2
BLOCKS = ("comp", "space")

ANGLES = 2.0 * np.pi * np.arange(ND) / ND
COS = [float(v) for v in np.cos(ANGLES)]
SIN = [float(v) for v in np.sin(ANGLES)]
HALF = 2.0 * np.pi * (np.arange(ND) + 0.5) / ND
SPREAD = float(np.cos(np.pi / ND))
COS_FACE = [float(v) * SPREAD for v in np.cos(HALF)]
SIN_FACE = [float(v) * SPREAD for v in np.sin(HALF)]

UPWARD = list(range(28, 36)) + list(range(0, 10))
DOWNWARD = list(range(10, 28))
CLASSES = 10

ONE = ND + 18
TWO = 2 * ND + 22 + 18
THIRD = 2 * ND
FOURTH = THIRD + 22


def places_one(row, d):
    up = d in UPWARD
    slot = (d + 8) % ND if up else d - 10
    if row == 3:
        return [(0, d)]
    if row == 0:
        return [(1, d)]
    if row == 2:
        return [(0, ND + slot)] if up else [(2, 18 + slot)]
    return [(2, slot)] if up else [(1, ND + slot)]


def places_two(row, d):
    up = d in UPWARD
    found = [(0, (3 - row) * ND + d)] if row >= 2 else [(1, row * ND + d)]
    if row == 1 and (d + 10) % ND < 22:
        found.append((0, THIRD + (d + 10) % ND))
    if row == 2 and 8 <= d < 30:
        found.append((1, THIRD + d - 8))
    if row == 0 and up:
        found.append((0, FOURTH + (d + 8) % ND))
    if row == 3 and not up:
        found.append((1, FOURTH + d - 10))
    return found


def pick_row(strip, row):
    index = lax.broadcasted_iota(jnp.int32, strip.shape, 0)
    return jnp.sum(jnp.where(index == row, strip, 0.0), axis=0, keepdims=True)


def column_of(row_values, first, count):
    size = row_values.shape[1]
    shape = (count, size)
    chosen = (
        lax.broadcasted_iota(jnp.int32, shape, 0) + first
        == lax.broadcasted_iota(jnp.int32, shape, 1)
    )
    return jnp.sum(jnp.where(chosen, row_values, 0.0), axis=1, keepdims=True)


def fetch(pairs, sems):
    copies = [pltpu.make_async_copy(src, dst, sems.at[i]) for i, (src, dst) in enumerate(pairs)]
    for copy in copies:
        copy.start()
    return copies


def run_copies(pairs, sems):
    for copy in fetch(pairs, sems):
        copy.wait()


def by_parity(odd, even_way, odd_way):
    pl.when(jnp.logical_not(odd))(even_way)
    pl.when(odd)(odd_way)


def source_kernel(chunk, freqs, last, comps, *refs):
    refs = list(refs)
    rows = 4
    block = refs.pop(0)[0]
    spectrum, wind, coupling, growth_in, dissipation_in, mask_in, index_in = (
        refs.pop(0) for _ in range(7)
    )
    if last:
        tables_in = [refs.pop(0) for _ in range(3)]
    even_out, odd_out = refs.pop(0), refs.pop(0)
    if last:
        kit_out = refs.pop(0)
    outs = [refs.pop(0) for _ in range(2)]
    spec, wind_ref, operator, growth_ref, dissipation_ref, rounded, mixed = refs[:7]
    mask_ref, index_ref, sems = refs[7:10]
    span = freqs * ND
    pairs = [(spectrum.at[:, pl.ds(r * LANES, LANES)], spec.at[r]) for r in range(rows)]
    pairs += [
        (coupling.at[pl.ds(chunk * span, span), :], operator),
        (wind, wind_ref),
        (growth_in, growth_ref),
        (dissipation_in, dissipation_ref),
        (mask_in, mask_ref),
        (index_in, index_ref),
    ]
    if last:
        kit = refs[10]
        depths_ref, speed_ref, refraction_ref = refs[11:]
        pairs += list(zip(tables_in, (depths_ref, speed_ref, refraction_ref)))
    copies = fetch(pairs, sems)
    for r in range(rows):
        copies[r].wait()
        rounded[:, r * LANES : (r + 1) * LANES] = spec[r].astype(jnp.bfloat16)
    for copy in copies[rows:]:
        copy.wait()
    nonlinear = jnp.dot(operator[...], rounded[...], preferred_element_type=jnp.float32)
    for r in range(rows):
        mixed[r] = nonlinear[:, r * LANES : (r + 1) * LANES]
    components = spec.shape[1]
    growth = column_of(growth_ref[...], chunk * freqs, freqs)
    dissipation = column_of(dissipation_ref[...], chunk * freqs, freqs)
    tiles = freqs // TILE
    for r in range(rows):
        average = jnp.sum(spec[r], axis=0, keepdims=True) * (1.0 / components)
        limited = average / (average + 1.0)
        wind_x = jnp.broadcast_to(wind_ref[0:1, r * LANES : (r + 1) * LANES], (TILE, LANES))
        wind_y = jnp.broadcast_to(wind_ref[1:2, r * LANES : (r + 1) * LANES], (TILE, LANES))
        grow = []
        damp = []
        for t in range(tiles):
            part = slice(t * TILE, (t + 1) * TILE)
            grow.append(jnp.broadcast_to(growth[part], (TILE, LANES)))
            damp.append(dissipation[part] * limited)
        for d in range(ND):
            forcing = jnp.maximum(COS[d] * wind_x + SIN[d] * wind_y, 0.0)
            squared = forcing * forcing
            for t in range(tiles):
                base = (chunk * freqs + t * TILE) * ND + d
                energy = spec[r, pl.ds(base, TILE, stride=ND), :]
                extra = mixed[r, pl.ds(t * TILE * ND + d, TILE, stride=ND), :]
                value = energy + (grow[t] * squared - damp[t]) * energy + 0.25 * extra
                for which, slot in places_two(r, d):
                    outs[which][slot, t * TILE : (t + 1) * TILE, :] = value
    first = lax.rem(block, comps) * rows
    mask = mask_ref[...].astype(jnp.float32)
    index = index_ref[...].astype(jnp.float32)
    leaving = []
    if chunk == 0:
        for out, row in ((outs[0], first + rows - 3), (outs[1], first)):
            for k in range(3):
                out[TWO, k : k + 1, :] = pick_row(mask, row + k)
                out[TWO, 3 + k : 4 + k, :] = pick_row(index, row + k)
            out[TWO, 6:, :] = jnp.zeros((freqs - 6, LANES), jnp.float32)
    if last:
        count, levels = speed_ref.shape
        kit[...] = jnp.zeros_like(kit)
        kit[:count, :levels] = speed_ref[...]
        kit[count : 2 * count, :levels] = refraction_ref[...]
        kit[2 * count : 2 * count + 1, :levels] = depths_ref[...]
        for r in range(rows):
            kit[2 * count + TILE + r, :] = pick_row(mask, first + r)[0]
            kit[2 * count + TILE + rows + r, :] = pick_row(index, first + r)[0]
        leaving.append((kit, kit_out))
    by_parity(
        lax.rem(block, 2) == 1,
        lambda: run_copies([(outs[0], even_out), (outs[1], odd_out)] + leaving, sems),
        lambda: run_copies([(outs[1], even_out), (outs[0], odd_out)] + leaving, sems),
    )


def weights(courant):
    half = 0.5 * courant
    square = courant * half
    curve = (half - courant * square) * (1.0 / 3.0)
    rising = half + square
    falling = half - square
    return rising + (curve + curve), falling - curve, curve


def coast_kernel(
    count, block_ref, even_ref, odd_ref, kit_ref, face_x, face_y, turn_ref, land_ref, slope_by
):
    rows = 4
    tables = kit_ref[: 2 * count + TILE, :]
    odd = lax.rem(block_ref[0], 2) == 1
    even, odds = even_ref[TWO, :TILE, :], odd_ref[TWO, :TILE, :]
    low, high = jnp.where(odd, even, odds), jnp.where(odd, odds, even)
    masks = [low[k : k + 1] for k in range(3)]
    levels = [low[3 + k : 4 + k] for k in range(3)]
    for r in range(rows):
        row = 2 * count + TILE + r
        masks.append(kit_ref[row : row + 1, :])
        levels.append(kit_ref[row + rows : row + rows + 1, :])
    masks += [high[k : k + 1] for k in range(3)]
    levels += [high[3 + k : 4 + k] for k in range(3)]
    wanted = jnp.concatenate(levels, axis=1)
    entry = lax.broadcasted_iota(jnp.int32, (LANES, wanted.shape[1]), 0).astype(jnp.float32)
    onehot = (entry == wanted).astype(jnp.float32)
    looked = jnp.dot(
        tables, onehot, precision=lax.Precision.HIGHEST, preferred_element_type=jnp.float32
    )
    speeds = looked[:count]
    turns = looked[count : 2 * count]
    depth = looked[2 * count : 2 * count + 1]

    def at(values, i):
        return values[:, i * LANES : (i + 1) * LANES]

    heights = [at(depth, i) * masks[i] for i in range(rows + 6)]
    for face in range(rows + 5):
        weight = 0.5 * (masks[face] * masks[face + 1])
        face_x[face] = (at(speeds, face) + at(speeds, face + 1)) * weight
    lane = lax.broadcasted_iota(jnp.int32, (1, LANES), 1)
    for r in range(rows + 4):
        mask = masks[r + 1]
        after = jnp.where(lane < LANES - 1, pltpu.roll(mask, LANES - 1, 1), 0.0)
        speed = at(speeds, r + 1)
        face_y[r] = (speed + pltpu.roll(speed, LANES - 1, 1)) * (0.5 * (mask * after))
        slope_x = 0.5 * (heights[r + 2] - heights[r])
        height = heights[r + 1]
        next_height = jnp.where(lane < LANES - 1, pltpu.roll(height, LANES - 1, 1), 0.0)
        last_height = jnp.where(lane > 0, pltpu.roll(height, 1, 1), 0.0)
        slope_y = 0.5 * (next_height - last_height)
        turn = at(turns, r + 1)
        slope_by[2 * r] = turn * slope_x
        slope_by[2 * r + 1] = turn * slope_y
        land_ref[r] = jnp.broadcast_to(mask, (TILE, LANES))

    @pl.loop(0, count // TILE)
    def _(t):
        part = pl.ds(pl.multiple_of(t * TILE, TILE), TILE)

        @pl.loop(0, rows + 4)
        def _(r):
            turn_x = slope_by[2 * r, part, :]
            turn_y = slope_by[2 * r + 1, part, :]
            for d in range(ND // 2):
                turn_ref[t, r * (ND // 2) + d] = turn_x * SIN_FACE[d] - turn_y * COS_FACE[d]


def shift_rows_columns(
    part, first, last, cells_of, moved, x_ref, y_ref, base, trig, j, members, put
):
    along_x = {
        k: weights(x_ref[base + k, part, :] * trig[0, j]) for k in range(first, last + 2)
    }
    for i, (d, _, up, _) in enumerate(members):
        cell = functools.partial(cells_of, d)
        if up:
            cells = {r: cell(r) for r in range(first - 2, last + 2)}
            faces = {
                k: a * cells[k - 1] + b * cells[k] - c * cells[k - 2]
                for k, (a, b, c) in along_x.items()
            }
            for r in range(first, last + 1):
                moved[i, r - first] = cells[r] - (faces[r + 1] - faces[r])
        else:
            cells = {r: cell(r) for r in range(first - 1, last + 3)}
            faces = {
                k: a * cells[k] + b * cells[k - 1] - c * cells[k + 1]
                for k, (a, b, c) in along_x.items()
            }
            for r in range(first, last + 1):
                moved[i, r - first] = cells[r] + (faces[r + 1] - faces[r])
    lanes = lax.broadcasted_iota(jnp.int32, (TILE, LANES), 1)
    not_first = (lanes != 0).astype(jnp.float32)
    not_last = (lanes != LANES - 2).astype(jnp.float32)
    for r in range(first, last + 1):
        near, far, curve = weights(y_ref[base + r, part, :] * trig[1, j])
        curve_up = curve * not_first
        curve_down = curve * not_last
        for i, (_, d, _, to_higher) in enumerate(members):
            here = moved[i, r - first]
            after = pltpu.roll(here, LANES - 1, 1)
            if to_higher:
                before = pltpu.roll(here, 1, 1)
                face = near * here + far * after - curve_up * before
                result = here - (face - pltpu.roll(face, 1, 1))
            else:
                beyond = pltpu.roll(here, LANES - 2, 1)
                face = near * after + far * here - curve_down * beyond
                result = here + (face - pltpu.roll(face, 1, 1))
            put(r, d, result)


def every_class(tiles, one_class):
    @pl.loop(0, CLASSES)
    def _(j):
        single = jnp.logical_or(j == 0, j == 9)
        rising = jnp.where(j == 0, 0, ND - j)
        members = [
            (j, j, True, True),
            (rising, jnp.where(single, ND, rising), True, False),
            (18 - j, jnp.where(j == 9, ND, 18 - j), False, True),
            (18 + j, jnp.where(j == 0, ND, 18 + j), False, False),
        ]
        for t in range(tiles):
            one_class(t, j, members)


def turn_rows(jobs):
    half_turn = ND // 2

    def slope(read, i):
        return read((i + 1) % ND) - read(i % ND)

    def pair(read, turning, d, known):
        courant = turning(d)
        half = 0.5 * courant
        spread = (1.0 / 3.0) - courant * (courant * (1.0 / 3.0))
        positive = courant >= 0.0
        faces = []
        following = []
        for side in range(2):
            own = d + side * half_turn
            rise, bend = known[side]
            next_rise = slope(read, own + 1)
            next_bend = next_rise - rise
            total = read(own) + read((own + 1) % ND)
            if side == 0:
                chosen = jnp.where(positive, bend, next_bend)
                faces.append(half * ((total - courant * rise) - spread * chosen))
            else:
                chosen = jnp.where(positive, next_bend, bend)
                faces.append(half * ((total + courant * rise) - spread * chosen))
            following.append((next_rise, next_bend))
        return faces, following

    def known_at(read, d):
        found = []
        for side in range(2):
            own = d + side * half_turn
            rise = slope(read, own)
            found.append((rise, rise - slope(read, own - 1)))
        return found

    states = []
    for read, turning, _, _ in jobs:
        ends, following = pair(read, turning, half_turn - 1, known_at(read, half_turn - 1))
        states.append((ends, [0.0 - ends[1], 0.0 - ends[0]], [following[1], following[0]]))
    for d in range(half_turn):
        for i, (read, turning, land, put) in enumerate(jobs):
            ends, previous, known = states[i]
            if d == half_turn - 1:
                current = ends
            else:
                current, known = pair(read, turning, d, known)
            put(d, (read(d) - (current[0] - previous[0])) * land)
            own = d + half_turn
            put(own, (read(own) + (current[1] - previous[1])) * land)
            states[i] = (ends, current, known)


def set_trig(trig):
    for j in range(CLASSES):
        trig[0, j] = abs(COS[j])
        trig[1, j] = abs(SIN[j])


def two_steps_kernel(chunk, freqs, *refs):
    block_ref, even_own, odd_own, even_ref, odd_ref, x_ref, y_ref, turn_ref, land_ref = refs[:9]
    even_out, odd_out, rest_out = refs[9:12]
    cells, work, moved, trig = refs[12:]
    odd = lax.rem(block_ref[0], 2) == 1
    tiles = freqs // TILE
    half_turn = ND // 2
    set_trig(trig)
    parts = [slice(t * TILE, (t + 1) * TILE) for t in range(tiles)]

    def gather(up_ref, down_ref, low_ref, high_ref):
        @pl.loop(0, ND)
        def _(d):
            for t, part in enumerate(parts):
                for k in range(2):
                    cells[0, t, 3 - k, d] = low_ref[k * ND + d, part, :]
                    cells[0, t, 4 + k, d] = down_ref[k * ND + d, part, :]
                    cells[0, t, 7 - k, d] = up_ref[k * ND + d, part, :]
                    cells[0, t, 8 + k, d] = high_ref[k * ND + d, part, :]

        @pl.loop(0, 22)
        def _(i):
            for t, part in enumerate(parts):
                cells[0, t, 1, lax.rem(i + 26, ND)] = low_ref[THIRD + i, part, :]
                cells[0, t, 10, i + 8] = high_ref[THIRD + i, part, :]

        @pl.loop(0, 18)
        def _(i):
            for t, part in enumerate(parts):
                cells[0, t, 0, lax.rem(i + 28, ND)] = low_ref[FOURTH + i, part, :]
                cells[0, t, 11, i + 10] = high_ref[FOURTH + i, part, :]

    by_parity(
        odd,
        lambda: gather(even_own, odd_own, odd_ref, even_ref),
        lambda: gather(odd_own, even_own, even_ref, odd_ref),
    )

    @pl.loop(0, 3)
    def _(stage):
        source = stage // 2
        base = jnp.where(stage == 0, 2, jnp.where(stage == 1, 6, 4))

        def one_class(t, j, members):
            def cell(d, r):
                return cells[source, t, base + r, d]

            def put(r, d, value):
                work[t, r, d] = value

            table = pl.ds(chunk * freqs + t * TILE, TILE)
            shift_rows_columns(
                table, 0, 3, cell, moved.at[t], x_ref, y_ref, base - 2, trig, j, members, put
            )

        every_class(tiles, one_class)

        @pl.loop(0, tiles * 4)
        def _(i):
            t = i // 4
            r = lax.rem(i, 4)

            def put(d, value):
                cells[1 - source, t, base + r, d] = value

            turn_rows(
                [
                    (
                        lambda d: work[t, r, d],
                        lambda d: turn_ref[chunk * tiles + t, (base - 2 + r) * half_turn + d],
                        land_ref[base - 2 + r],
                        put,
                    )
                ]
            )

    def hand_out(up_out, down_out):
        @pl.loop(0, ND)
        def _(d):
            for t, part in enumerate(parts):
                up_out[d, part, :] = cells[0, t, 7, d]
                down_out[d, part, :] = cells[0, t, 4, d]

        @pl.loop(0, half_turn)
        def _(i):
            upward = lax.rem(i + 28, ND)
            for t, part in enumerate(parts):
                up_out[ND + i, part, :] = cells[0, t, 6, upward]
                down_out[ND + i, part, :] = cells[0, t, 5, i + 10]
                rest_out[i, part, :] = cells[0, t, 5, upward]
                rest_out[half_turn + i, part, :] = cells[0, t, 6, i + 10]

    by_parity(odd, lambda: hand_out(even_out, odd_out), lambda: hand_out(odd_out, even_out))


def last_step_kernel(chunk, freqs, *refs):
    refs = list(refs)
    odd = lax.rem(refs.pop(0)[0], 2) == 1
    even_own, odd_own, rest_ref, even_ref, odd_ref = (refs.pop(0) for _ in range(5))
    x_ref, y_ref, turn_ref, land_ref = (refs.pop(0) for _ in range(4))
    if chunk:
        refs.pop(0)
    out_ref, cells, work, moved, packed, trig, sems = refs
    rows = 4
    tiles = freqs // TILE
    half_turn = ND // 2
    span = freqs * ND
    set_trig(trig)
    parts = [slice(t * TILE, (t + 1) * TILE) for t in range(tiles)]

    def gather(up_ref, down_ref, low_ref, high_ref):
        @pl.loop(0, ND)
        def _(d):
            for t, part in enumerate(parts):
                cells[t, 1, d] = low_ref[d, part, :]
                cells[t, 2, d] = down_ref[d, part, :]
                cells[t, 5, d] = up_ref[d, part, :]
                cells[t, 6, d] = high_ref[d, part, :]

        @pl.loop(0, half_turn)
        def _(i):
            upward = lax.rem(i + 28, ND)
            for t, part in enumerate(parts):
                cells[t, 0, upward] = low_ref[ND + i, part, :]
                cells[t, 3, upward] = rest_ref[i, part, :]
                cells[t, 4, upward] = up_ref[ND + i, part, :]
                cells[t, 3, i + 10] = down_ref[ND + i, part, :]
                cells[t, 4, i + 10] = rest_ref[half_turn + i, part, :]
                cells[t, 7, i + 10] = high_ref[ND + i, part, :]

    by_parity(
        odd,
        lambda: gather(even_own, odd_own, odd_ref, even_ref),
        lambda: gather(odd_own, even_own, even_ref, odd_ref),
    )

    def only_pass(t, j, members):
        def cell(d, r):
            return cells[t, r + 2, d]

        def put(r, d, value):
            work[t, r, d] = value

        table = pl.ds(chunk * freqs + t * TILE, TILE)
        shift_rows_columns(
            table, 0, 3, cell, moved.at[t], x_ref, y_ref, 2, trig, j, members, put
        )

    every_class(tiles, only_pass)

    @pl.loop(0, tiles * 4)
    def _(i):
        t = i // 4
        r = lax.rem(i, 4)

        def put(d, value):
            packed[r, pl.ds(t * (TILE * ND) + d, TILE, stride=ND), :] = value

        turn_rows(
            [
                (
                    lambda d: work[t, r, d],
                    lambda d: turn_ref[chunk * tiles + t, (r + 2) * half_turn + d],
                    land_ref[r + 2],
                    put,
                )
            ]
        )

    run_copies(
        [
            (packed.at[r], out_ref.at[pl.ds(chunk * span, span), pl.ds(r * LANES, LANES)])
            for r in range(rows)
        ],
        sems,
    )


def cost(flops, size):
    return pl.CostEstimate(flops=flops, bytes_accessed=size, transcendentals=0)


def params(limit):
    return pltpu.CompilerParams(vmem_limit_bytes=limit * 1024 * 1024)


def per_device(
    spectrum,
    wind_field,
    coupling,
    growth,
    dissipation,
    group_speed,
    refraction,
    depths,
    sea_mask,
    depth_index,
):
    components, points = spectrum.shape
    nfreq = growth.shape[0]
    levels = depths.shape[0]
    rows = points // LANES
    freqs = nfreq // CHUNKS
    span = freqs * ND
    comps, strips = lax.axis_size("comp"), lax.axis_size("space")
    order = [c * strips + s for s in range(strips) for c in range(comps)]
    steps = list(zip(order[:-1], order[1:]))
    even_swaps = [swap for i, j in steps[0::2] for swap in ((i, j), (j, i))]
    odd_swaps = [swap for i, j in steps[1::2] for swap in ((i, j), (j, i))]
    block_index = lax.axis_index("space") * comps + lax.axis_index("comp")
    block_index = block_index.astype(jnp.int32).reshape(1)
    scalar = pl.BlockSpec(memory_space=pltpu.SMEM)
    near = pl.BlockSpec(memory_space=pltpu.VMEM)
    far = pl.BlockSpec(memory_space=pltpu.HBM)
    growth = growth.reshape(1, nfreq)
    dissipation = dissipation.reshape(1, nfreq)
    depths = depths.reshape(1, levels)

    def block(*shape):
        return jax.ShapeDtypeStruct(shape, jnp.float32)

    def like(array):
        return pltpu.VMEM(array.shape, array.dtype)

    def tiles(count):
        return block(count, freqs, LANES)

    def source(chunk):
        last = chunk == CHUNKS - 1
        shapes = [tiles(TWO + (1 if chunk == 0 else 0))] * 2
        operands = [spectrum, wind_field, coupling, growth, dissipation, sea_mask, depth_index]
        scratch = [like(shape) for shape in shapes] + [
            pltpu.VMEM((rows, components, LANES), jnp.float32),
            like(wind_field),
            pltpu.VMEM((span, components), jnp.bfloat16),
            like(growth),
            like(dissipation),
            pltpu.VMEM((components, points), jnp.bfloat16),
            pltpu.VMEM((rows, span, LANES), jnp.float32),
            like(sea_mask),
            like(depth_index),
            pltpu.SemaphoreType.DMA((14,)),
        ]
        if last:
            shapes.append(block(2 * nfreq + 2 * TILE, LANES))
            more = [depths, group_speed, refraction]
            operands += more
            scratch += [like(shapes[2])] + [like(a) for a in more]
        return pl.pallas_call(
            functools.partial(source_kernel, chunk, freqs, last, comps),
            in_specs=[scalar] + [far] * len(operands),
            out_specs=[far] * len(shapes),
            out_shape=shapes,
            scratch_shapes=scratch,
            compiler_params=params(57 if chunk else 63),
            cost_estimate=cost(2 * span * components * points, 4 * components * points),
            name="source_terms",
        )(block_index, *operands)

    def coast(even, odd, kit):
        shapes = [
            block(rows + 5, nfreq, LANES),
            block(rows + 4, nfreq, LANES),
            block(nfreq // TILE, (rows + 4) * (ND // 2), TILE, LANES),
            block(rows + 4, TILE, LANES),
        ]
        return pl.pallas_call(
            functools.partial(coast_kernel, nfreq),
            in_specs=[scalar] + [near] * 3,
            out_specs=[near] * len(shapes),
            out_shape=shapes,
            scratch_shapes=[pltpu.VMEM((2 * (rows + 4), nfreq, LANES), jnp.float32)],
            compiler_params=params(24),
            cost_estimate=cost(ND * rows * nfreq * LANES, 4 * ND * rows * nfreq * LANES),
            name="coast_tables",
        )(block_index, even, odd, kit)

    def exchange(even, odd):
        odd = lax.ppermute(odd, BLOCKS, odd_swaps)
        return lax.ppermute(even, BLOCKS, even_swaps), odd

    work = pltpu.VMEM((freqs // TILE, rows, ND + 1, TILE, LANES), jnp.float32)

    passed = pltpu.VMEM((freqs // TILE, 4, rows, TILE, LANES), jnp.float32)

    trig = pltpu.SMEM((2, CLASSES), jnp.float32)

    def two_steps(chunk, state, halo, tables):
        operands = [block_index, *state, *halo, *tables]
        shapes = [tiles(ONE), tiles(ONE), tiles(ND)]
        return pl.pallas_call(
            functools.partial(two_steps_kernel, chunk, freqs),
            in_specs=[scalar] + [near] * (len(operands) - 1),
            out_specs=[near] * len(shapes),
            out_shape=shapes,
            scratch_shapes=[
                pltpu.VMEM((2, freqs // TILE, rows + 8, ND, TILE, LANES), jnp.float32),
                work,
                passed,
                trig,
            ],
            compiler_params=params(24),
            cost_estimate=cost(3 * 40 * span * points, 4 * 4 * span * points),
            name="two_substeps",
        )(*operands)

    def last_step(chunk, state, halo, tables, out):
        operands = [block_index, *state, *halo, *tables]
        specs = [scalar] + [near] * (len(operands) - 1)
        aliases = {}
        if out is not None:
            aliases = {len(operands): 0}
            operands.append(out)
            specs.append(far)
        return pl.pallas_call(
            functools.partial(last_step_kernel, chunk, freqs),
            in_specs=specs,
            out_specs=far,
            out_shape=block(*spectrum.shape),
            scratch_shapes=[
                pltpu.VMEM((freqs // TILE, rows + 4, ND, TILE, LANES), jnp.float32),
                work,
                passed,
                pltpu.VMEM((rows, span, LANES), jnp.float32),
                trig,
                pltpu.SemaphoreType.DMA((rows,)),
            ],
            input_output_aliases=aliases,
            compiler_params=params(24),
            cost_estimate=cost(40 * span * points, 4 * 4 * span * points),
            name="last_substep",
        )(*operands)

    states = []
    halos = []
    for chunk in range(CHUNKS):
        even, odd, *kit = source(chunk)
        states.append((even, odd))
        halos.append(exchange(even, odd))
    tables = coast(*halos[0], *kit)
    for chunk in range(CHUNKS):
        states[chunk] = two_steps(chunk, states[chunk], halos[chunk], tables)
        halos[chunk] = exchange(*states[chunk][:2])
    out = None
    for chunk in range(CHUNKS):
        out = last_step(chunk, states[chunk], halos[chunk], tables, out)
    return out


def solution(mesh):
    in_specs = (
        P(None, ("comp", "space")),
        P(None, ("comp", "space")),
        P(),
        P(),
        P(),
        P(),
        P(),
        P(),
        P("space", None),
        P("space", None),
    )
    out_specs = P(None, ("comp", "space"))
    return jax.shard_map(
        per_device, mesh=mesh, in_specs=in_specs, out_specs=out_specs, check_vma=False
    )
```

```python
import functools

import jax
import jax.numpy as jnp
import numpy as np
from jax import lax
from jax.experimental import pallas as pl
from jax.experimental.pallas import tpu as pltpu
from jax.sharding import PartitionSpec as P

ND = 36
LANES = 128
TILE = 8
CHUNKS = 2
BLOCKS = ("comp", "space")

ANGLES = 2.0 * np.pi * np.arange(ND) / ND
COS = [float(v) for v in np.cos(ANGLES)]
SIN = [float(v) for v in np.sin(ANGLES)]
HALF = 2.0 * np.pi * (np.arange(ND) + 0.5) / ND
SPREAD = float(np.cos(np.pi / ND))
COS_FACE = [float(v) * SPREAD for v in np.cos(HALF)]
SIN_FACE = [float(v) * SPREAD for v in np.sin(HALF)]

UPWARD = list(range(28, 36)) + list(range(0, 10))
DOWNWARD = list(range(10, 28))
CLASSES = 10

ONE = ND + 18
TWO = 2 * ND + 22 + 18
THIRD = 2 * ND
FOURTH = THIRD + 22


def places_one(row, d):
    up = d in UPWARD
    slot = (d + 8) % ND if up else d - 10
    if row == 3:
        return [(0, d)]
    if row == 0:
        return [(1, d)]
    if row == 2:
        return [(0, ND + slot)] if up else [(2, 18 + slot)]
    return [(2, slot)] if up else [(1, ND + slot)]


def places_two(row, d):
    up = d in UPWARD
    found = [(0, (3 - row) * ND + d)] if row >= 2 else [(1, row * ND + d)]
    if row == 1 and (d + 10) % ND < 22:
        found.append((0, THIRD + (d + 10) % ND))
    if row == 2 and 8 <= d < 30:
        found.append((1, THIRD + d - 8))
    if row == 0 and up:
        found.append((0, FOURTH + (d + 8) % ND))
    if row == 3 and not up:
        found.append((1, FOURTH + d - 10))
    return found


def pick_row(strip, row):
    index = lax.broadcasted_iota(jnp.int32, strip.shape, 0)
    return jnp.sum(jnp.where(index == row, strip, 0.0), axis=0, keepdims=True)


def column_of(row_values, first, count):
    size = row_values.shape[1]
    shape = (count, size)
    chosen = (
        lax.broadcasted_iota(jnp.int32, shape, 0) + first
        == lax.broadcasted_iota(jnp.int32, shape, 1)
    )
    return jnp.sum(jnp.where(chosen, row_values, 0.0), axis=1, keepdims=True)


def fetch(pairs, sems):
    copies = [pltpu.make_async_copy(src, dst, sems.at[i]) for i, (src, dst) in enumerate(pairs)]
    for copy in copies:
        copy.start()
    return copies


def run_copies(pairs, sems):
    for copy in fetch(pairs, sems):
        copy.wait()


def by_parity(odd, even_way, odd_way):
    pl.when(jnp.logical_not(odd))(even_way)
    pl.when(odd)(odd_way)


def source_kernel(chunk, freqs, last, comps, *refs):
    refs = list(refs)
    rows = 4
    block = refs.pop(0)[0]
    spectrum, wind, coupling, growth_in, dissipation_in, mask_in, index_in = (
        refs.pop(0) for _ in range(7)
    )
    if last:
        tables_in = [refs.pop(0) for _ in range(3)]
    even_out, odd_out = refs.pop(0), refs.pop(0)
    if last:
        kit_out = refs.pop(0)
    outs = [refs.pop(0) for _ in range(2)]
    spec, wind_ref, operator, growth_ref, dissipation_ref, rounded, mixed = refs[:7]
    mask_ref, index_ref, sems, out_sems = refs[7:11]
    span = freqs * ND
    pairs = [(spectrum.at[:, pl.ds(r * LANES, LANES)], spec.at[r]) for r in range(rows)]
    pairs += [
        (coupling.at[pl.ds(chunk * span, span), :], operator),
        (wind, wind_ref),
        (growth_in, growth_ref),
        (dissipation_in, dissipation_ref),
        (mask_in, mask_ref),
        (index_in, index_ref),
    ]
    if last:
        kit = refs[11]
        depths_ref, speed_ref, refraction_ref = refs[12:]
        pairs += list(zip(tables_in, (depths_ref, speed_ref, refraction_ref)))
    copies = fetch(pairs, sems)
    components = spec.shape[1]
    tiles = freqs // TILE
    odd = lax.rem(block, 2) == 1

    def leave(number, which, start, count):
        part = pl.ds(start, count)

        def begin(to):
            pltpu.make_async_copy(outs[which].at[part], to.at[part], out_sems.at[number]).start()

        by_parity(
            odd,
            lambda: begin((even_out, odd_out)[which]),
            lambda: begin((odd_out, even_out)[which]),
        )
        return pltpu.make_async_copy(outs[which].at[part], even_out.at[part], out_sems.at[number])

    def work_on(r, growth, dissipation):
        average = jnp.sum(spec[r], axis=0, keepdims=True) * (1.0 / components)
        limited = average / (average + 1.0)
        wind_x = jnp.broadcast_to(wind_ref[0:1, r * LANES : (r + 1) * LANES], (TILE, LANES))
        wind_y = jnp.broadcast_to(wind_ref[1:2, r * LANES : (r + 1) * LANES], (TILE, LANES))
        grow = []
        damp = []
        for t in range(tiles):
            part = slice(t * TILE, (t + 1) * TILE)
            grow.append(jnp.broadcast_to(growth[part], (TILE, LANES)))
            damp.append(dissipation[part] * limited)
        for d in range(ND):
            forcing = jnp.maximum(COS[d] * wind_x + SIN[d] * wind_y, 0.0)
            squared = forcing * forcing
            for t in range(tiles):
                base = (chunk * freqs + t * TILE) * ND + d
                energy = spec[r, pl.ds(base, TILE, stride=ND), :]
                extra = mixed[r, pl.ds(t * TILE * ND + d, TILE, stride=ND), :]
                value = energy + (grow[t] * squared - damp[t]) * energy + 0.25 * extra
                for which, slot in places_two(r, d):
                    outs[which][slot, t * TILE : (t + 1) * TILE, :] = value

    leaving = []
    growth = dissipation = None
    for first_row in (0, 2):
        for r in (first_row, first_row + 1):
            copies[r].wait()
            rounded[:, r * LANES : (r + 1) * LANES] = spec[r].astype(jnp.bfloat16)
        if first_row == 0:
            for copy in copies[rows:]:
                copy.wait()
            growth = column_of(growth_ref[...], chunk * freqs, freqs)
            dissipation = column_of(dissipation_ref[...], chunk * freqs, freqs)
        both = slice(first_row * LANES, (first_row + 2) * LANES)
        nonlinear = jnp.dot(
            operator[...], rounded[:, both], preferred_element_type=jnp.float32
        )
        for r in (first_row, first_row + 1):
            mixed[r] = nonlinear[:, (r - first_row) * LANES : (r - first_row + 1) * LANES]
            work_on(r, growth, dissipation)
        if first_row == 0:
            leaving += [leave(0, 1, 0, THIRD), leave(1, 0, THIRD, TWO - THIRD)]
    leaving += [leave(2, 0, 0, THIRD), leave(3, 1, THIRD, TWO - THIRD)]
    first = lax.rem(block, comps) * rows
    mask = mask_ref[...].astype(jnp.float32)
    index = index_ref[...].astype(jnp.float32)
    if chunk == 0:
        for out, row in ((outs[0], first + rows - 3), (outs[1], first)):
            for k in range(3):
                out[TWO, k : k + 1, :] = pick_row(mask, row + k)
                out[TWO, 3 + k : 4 + k, :] = pick_row(index, row + k)
            out[TWO, 6:, :] = jnp.zeros((freqs - 6, LANES), jnp.float32)
        leaving += [leave(4, 0, TWO, 1), leave(5, 1, TWO, 1)]
    if last:
        count, levels = speed_ref.shape
        kit[...] = jnp.zeros_like(kit)
        kit[:count, :levels] = speed_ref[...]
        kit[count : 2 * count, :levels] = refraction_ref[...]
        kit[2 * count : 2 * count + 1, :levels] = depths_ref[...]
        for r in range(rows):
            kit[2 * count + TILE + r, :] = pick_row(mask, first + r)[0]
            kit[2 * count + TILE + rows + r, :] = pick_row(index, first + r)[0]
        run_copies([(kit, kit_out)], sems)
    for copy in leaving:
        copy.wait()


def weights(courant):
    half = 0.5 * courant
    square = courant * half
    curve = (half - courant * square) * (1.0 / 3.0)
    rising = half + square
    falling = half - square
    return rising + (curve + curve), falling - curve, curve


def coast_kernel(
    count, block_ref, even_ref, odd_ref, kit_ref, face_x, face_y, turn_ref, land_ref, slope_by
):
    rows = 4
    tables = kit_ref[: 2 * count + TILE, :]
    odd = lax.rem(block_ref[0], 2) == 1
    even, odds = even_ref[TWO, :TILE, :], odd_ref[TWO, :TILE, :]
    low, high = jnp.where(odd, even, odds), jnp.where(odd, odds, even)
    masks = [low[k : k + 1] for k in range(3)]
    levels = [low[3 + k : 4 + k] for k in range(3)]
    for r in range(rows):
        row = 2 * count + TILE + r
        masks.append(kit_ref[row : row + 1, :])
        levels.append(kit_ref[row + rows : row + rows + 1, :])
    masks += [high[k : k + 1] for k in range(3)]
    levels += [high[3 + k : 4 + k] for k in range(3)]
    wanted = jnp.concatenate(levels, axis=1)
    entry = lax.broadcasted_iota(jnp.int32, (LANES, wanted.shape[1]), 0).astype(jnp.float32)
    onehot = (entry == wanted).astype(jnp.float32)
    looked = jnp.dot(
        tables, onehot, precision=lax.Precision.HIGHEST, preferred_element_type=jnp.float32
    )
    speeds = looked[:count]
    turns = looked[count : 2 * count]
    depth = looked[2 * count : 2 * count + 1]

    def at(values, i):
        return values[:, i * LANES : (i + 1) * LANES]

    heights = [at(depth, i) * masks[i] for i in range(rows + 6)]
    for face in range(rows + 5):
        weight = 0.5 * (masks[face] * masks[face + 1])
        face_x[face] = (at(speeds, face) + at(speeds, face + 1)) * weight
    lane = lax.broadcasted_iota(jnp.int32, (1, LANES), 1)
    for r in range(rows + 4):
        mask = masks[r + 1]
        after = jnp.where(lane < LANES - 1, pltpu.roll(mask, LANES - 1, 1), 0.0)
        speed = at(speeds, r + 1)
        face_y[r] = (speed + pltpu.roll(speed, LANES - 1, 1)) * (0.5 * (mask * after))
        slope_x = 0.5 * (heights[r + 2] - heights[r])
        height = heights[r + 1]
        next_height = jnp.where(lane < LANES - 1, pltpu.roll(height, LANES - 1, 1), 0.0)
        last_height = jnp.where(lane > 0, pltpu.roll(height, 1, 1), 0.0)
        slope_y = 0.5 * (next_height - last_height)
        turn = at(turns, r + 1)
        slope_by[2 * r] = turn * slope_x
        slope_by[2 * r + 1] = turn * slope_y
        land_ref[r] = jnp.broadcast_to(mask, (TILE, LANES))

    @pl.loop(0, count // TILE)
    def _(t):
        part = pl.ds(pl.multiple_of(t * TILE, TILE), TILE)

        @pl.loop(0, rows + 4)
        def _(r):
            turn_x = slope_by[2 * r, part, :]
            turn_y = slope_by[2 * r + 1, part, :]
            for d in range(ND // 2):
                turn_ref[t, r * (ND // 2) + d] = turn_x * SIN_FACE[d] - turn_y * COS_FACE[d]


def shift_rows_columns(
    part, first, last, cells_of, moved, x_ref, y_ref, base, trig, j, members, rows_of
):
    count = last - first + 1
    faces_x = x_ref.at[pl.ds(base + first, count + 1), part]
    faces_y = y_ref.at[pl.ds(base + first, count), part]
    along_x = {
        k: weights(faces_x[k - first] * trig[0, j]) for k in range(first, last + 2)
    }
    for i, (d, _, up, _) in enumerate(members):
        cell = cells_of(d)
        if up:
            cells = {r: cell[r - first + 2] for r in range(first - 2, last + 2)}
            faces = {
                k: a * cells[k - 1] + b * cells[k] - c * cells[k - 2]
                for k, (a, b, c) in along_x.items()
            }
            for r in range(first, last + 1):
                moved[i, r - first] = cells[r] - (faces[r + 1] - faces[r])
        else:
            cells = {r: cell[r - first + 2] for r in range(first - 1, last + 3)}
            faces = {
                k: a * cells[k] + b * cells[k - 1] - c * cells[k + 1]
                for k, (a, b, c) in along_x.items()
            }
            for r in range(first, last + 1):
                moved[i, r - first] = cells[r] + (faces[r + 1] - faces[r])
    lanes = lax.broadcasted_iota(jnp.int32, (TILE, LANES), 1)
    not_first = (lanes != 0).astype(jnp.float32)
    not_last = (lanes != LANES - 2).astype(jnp.float32)
    results = [rows_of(d) for _, d, _, _ in members]
    for r in range(first, last + 1):
        near, far, curve = weights(faces_y[r - first] * trig[1, j])
        curve_up = curve * not_first
        curve_down = curve * not_last
        for i, (_, _, _, to_higher) in enumerate(members):
            here = moved[i, r - first]
            after = pltpu.roll(here, LANES - 1, 1)
            if to_higher:
                before = pltpu.roll(here, 1, 1)
                face = near * here + far * after - curve_up * before
                result = here - (face - pltpu.roll(face, 1, 1))
            else:
                beyond = pltpu.roll(here, LANES - 2, 1)
                face = near * after + far * here - curve_down * beyond
                result = here + (face - pltpu.roll(face, 1, 1))
            results[i][r - first] = result


def every_class(tiles, one_class):
    @pl.loop(0, CLASSES)
    def _(j):
        single = jnp.logical_or(j == 0, j == 9)
        rising = jnp.where(j == 0, 0, ND - j)
        members = [
            (j, j, True, True),
            (rising, jnp.where(single, ND, rising), True, False),
            (18 - j, jnp.where(j == 9, ND, 18 - j), False, True),
            (18 + j, jnp.where(j == 0, ND, 18 + j), False, False),
        ]
        for t in range(tiles):
            one_class(t, j, members)


def turn_row(cells, turnings, land, out):
    half_turn = ND // 2

    def slope(i):
        return cells[(i + 1) % ND] - cells[i % ND]

    def pair(d, known):
        courant = turnings[d]
        half = 0.5 * courant
        spread = (1.0 / 3.0) - courant * (courant * (1.0 / 3.0))
        positive = courant >= 0.0
        faces = []
        following = []
        for side in range(2):
            own = d + side * half_turn
            rise, bend = known[side]
            next_rise = slope(own + 1)
            next_bend = next_rise - rise
            total = cells[own] + cells[(own + 1) % ND]
            if side == 0:
                chosen = jnp.where(positive, bend, next_bend)
                faces.append(half * ((total - courant * rise) - spread * chosen))
            else:
                chosen = jnp.where(positive, next_bend, bend)
                faces.append(half * ((total + courant * rise) - spread * chosen))
            following.append((next_rise, next_bend))
        return faces, following

    known = []
    for side in range(2):
        own = half_turn - 1 + side * half_turn
        rise = slope(own)
        known.append((rise, rise - slope(own - 1)))
    ends, following = pair(half_turn - 1, known)
    previous = [0.0 - ends[1], 0.0 - ends[0]]
    known = [following[1], following[0]]
    for d in range(half_turn):
        if d == half_turn - 1:
            current = ends
        else:
            current, known = pair(d, known)
        out[d] = (cells[d] - (current[0] - previous[0])) * land
        own = d + half_turn
        out[own] = (cells[own] + (current[1] - previous[1])) * land
        previous = current


def set_trig(trig):
    for j in range(CLASSES):
        trig[0, j] = abs(COS[j])
        trig[1, j] = abs(SIN[j])


def two_steps_kernel(chunk, freqs, *refs):
    block_ref, even_own, odd_own, even_ref, odd_ref, x_ref, y_ref, turn_ref, land_ref = refs[:9]
    even_out, odd_out, rest_out = refs[9:12]
    cells, work, moved, trig = refs[12:]
    odd = lax.rem(block_ref[0], 2) == 1
    tiles = freqs // TILE
    half_turn = ND // 2
    set_trig(trig)
    parts = [slice(t * TILE, (t + 1) * TILE) for t in range(tiles)]

    def gather(up_ref, down_ref, low_ref, high_ref):
        @pl.loop(0, ND)
        def _(d):
            for t, part in enumerate(parts):
                for k in range(2):
                    cells[0, t, 3 - k, d] = low_ref[k * ND + d, part, :]
                    cells[0, t, 4 + k, d] = down_ref[k * ND + d, part, :]
                    cells[0, t, 7 - k, d] = up_ref[k * ND + d, part, :]
                    cells[0, t, 8 + k, d] = high_ref[k * ND + d, part, :]

        @pl.loop(0, 22)
        def _(i):
            for t, part in enumerate(parts):
                cells[0, t, 1, lax.rem(i + 26, ND)] = low_ref[THIRD + i, part, :]
                cells[0, t, 10, i + 8] = high_ref[THIRD + i, part, :]

        @pl.loop(0, 18)
        def _(i):
            for t, part in enumerate(parts):
                cells[0, t, 0, lax.rem(i + 28, ND)] = low_ref[FOURTH + i, part, :]
                cells[0, t, 11, i + 10] = high_ref[FOURTH + i, part, :]

    by_parity(
        odd,
        lambda: gather(even_own, odd_own, odd_ref, even_ref),
        lambda: gather(odd_own, even_own, even_ref, odd_ref),
    )

    @pl.loop(0, 3)
    def _(stage):
        source = stage // 2
        base = jnp.where(stage == 0, 2, jnp.where(stage == 1, 6, 4))

        def one_class(t, j, members):
            def cell(d):
                return cells.at[source, t, pl.ds(base - 2, 8), d]

            def put(d):
                return work.at[t, :, d]

            table = pl.ds(chunk * freqs + t * TILE, TILE)
            shift_rows_columns(
                table, 0, 3, cell, moved.at[t], x_ref, y_ref, base - 2, trig, j, members, put
            )

        every_class(tiles, one_class)

        @pl.loop(0, tiles * 4)
        def _(i):
            t = i // 4
            r = lax.rem(i, 4)
            turning = pl.ds((base - 2 + r) * half_turn, half_turn)
            turn_row(
                work.at[t, r],
                turn_ref.at[chunk * tiles + t, turning],
                land_ref[base - 2 + r],
                cells.at[1 - source, t, base + r],
            )

    def hand_out(up_out, down_out):
        @pl.loop(0, ND)
        def _(d):
            for t, part in enumerate(parts):
                up_out[d, part, :] = cells[0, t, 7, d]
                down_out[d, part, :] = cells[0, t, 4, d]

        @pl.loop(0, half_turn)
        def _(i):
            upward = lax.rem(i + 28, ND)
            for t, part in enumerate(parts):
                up_out[ND + i, part, :] = cells[0, t, 6, upward]
                down_out[ND + i, part, :] = cells[0, t, 5, i + 10]
                rest_out[i, part, :] = cells[0, t, 5, upward]
                rest_out[half_turn + i, part, :] = cells[0, t, 6, i + 10]

    by_parity(odd, lambda: hand_out(even_out, odd_out), lambda: hand_out(odd_out, even_out))


def last_step_kernel(chunk, freqs, *refs):
    refs = list(refs)
    odd = lax.rem(refs.pop(0)[0], 2) == 1
    even_own, odd_own, rest_ref, even_ref, odd_ref = (refs.pop(0) for _ in range(5))
    x_ref, y_ref, turn_ref, land_ref = (refs.pop(0) for _ in range(4))
    if chunk:
        refs.pop(0)
    out_ref, cells, work, moved, packed, trig, sems = refs
    rows = 4
    tiles = freqs // TILE
    half_turn = ND // 2
    span = freqs * ND
    set_trig(trig)
    parts = [slice(t * TILE, (t + 1) * TILE) for t in range(tiles)]

    def gather(up_ref, down_ref, low_ref, high_ref):
        @pl.loop(0, ND)
        def _(d):
            for t, part in enumerate(parts):
                cells[t, 1, d] = low_ref[d, part, :]
                cells[t, 2, d] = down_ref[d, part, :]
                cells[t, 5, d] = up_ref[d, part, :]
                cells[t, 6, d] = high_ref[d, part, :]

        @pl.loop(0, half_turn)
        def _(i):
            upward = lax.rem(i + 28, ND)
            for t, part in enumerate(parts):
                cells[t, 0, upward] = low_ref[ND + i, part, :]
                cells[t, 3, upward] = rest_ref[i, part, :]
                cells[t, 4, upward] = up_ref[ND + i, part, :]
                cells[t, 3, i + 10] = down_ref[ND + i, part, :]
                cells[t, 4, i + 10] = rest_ref[half_turn + i, part, :]
                cells[t, 7, i + 10] = high_ref[ND + i, part, :]

    by_parity(
        odd,
        lambda: gather(even_own, odd_own, odd_ref, even_ref),
        lambda: gather(odd_own, even_own, even_ref, odd_ref),
    )

    def only_pass(t, j, members):
        def cell(d):
            return cells.at[t, :, d]

        def put(d):
            return work.at[t, :, d]

        table = pl.ds(chunk * freqs + t * TILE, TILE)
        shift_rows_columns(
            table, 0, 3, cell, moved.at[t], x_ref, y_ref, 2, trig, j, members, put
        )

    every_class(tiles, only_pass)

    @pl.loop(0, tiles * 4)
    def _(i):
        t = i // 4
        r = lax.rem(i, 4)

        turn_row(
            work.at[t, r],
            turn_ref.at[chunk * tiles + t, pl.ds((r + 2) * half_turn, half_turn)],
            land_ref[r + 2],
            cells.at[t, r + 2],
        )

    @pl.loop(0, ND)
    def _(d):
        for t in range(tiles):
            for r in range(rows):
                place = pl.ds(t * (TILE * ND) + d, TILE, stride=ND)
                packed[r, place, :] = cells[t, r + 2, d]

    run_copies(
        [
            (packed.at[r], out_ref.at[pl.ds(chunk * span, span), pl.ds(r * LANES, LANES)])
            for r in range(rows)
        ],
        sems,
    )


def cost(flops, size):
    return pl.CostEstimate(flops=flops, bytes_accessed=size, transcendentals=0)


def params(limit):
    return pltpu.CompilerParams(vmem_limit_bytes=limit * 1024 * 1024)


def per_device(
    spectrum,
    wind_field,
    coupling,
    growth,
    dissipation,
    group_speed,
    refraction,
    depths,
    sea_mask,
    depth_index,
):
    components, points = spectrum.shape
    nfreq = growth.shape[0]
    levels = depths.shape[0]
    rows = points // LANES
    freqs = nfreq // CHUNKS
    span = freqs * ND
    comps, strips = lax.axis_size("comp"), lax.axis_size("space")
    order = [c * strips + s for s in range(strips) for c in range(comps)]
    steps = list(zip(order[:-1], order[1:]))
    even_swaps = [swap for i, j in steps[0::2] for swap in ((i, j), (j, i))]
    odd_swaps = [swap for i, j in steps[1::2] for swap in ((i, j), (j, i))]
    block_index = lax.axis_index("space") * comps + lax.axis_index("comp")
    block_index = block_index.astype(jnp.int32).reshape(1)
    scalar = pl.BlockSpec(memory_space=pltpu.SMEM)
    near = pl.BlockSpec(memory_space=pltpu.VMEM)
    far = pl.BlockSpec(memory_space=pltpu.HBM)
    growth = growth.reshape(1, nfreq)
    dissipation = dissipation.reshape(1, nfreq)
    depths = depths.reshape(1, levels)

    def block(*shape):
        return jax.ShapeDtypeStruct(shape, jnp.float32)

    def like(array):
        return pltpu.VMEM(array.shape, array.dtype)

    def tiles(count):
        return block(count, freqs, LANES)

    def source(chunk):
        last = chunk == CHUNKS - 1
        shapes = [tiles(TWO + (1 if chunk == 0 else 0))] * 2
        operands = [spectrum, wind_field, coupling, growth, dissipation, sea_mask, depth_index]
        scratch = [like(shape) for shape in shapes] + [
            pltpu.VMEM((rows, components, LANES), jnp.float32),
            like(wind_field),
            pltpu.VMEM((span, components), jnp.bfloat16),
            like(growth),
            like(dissipation),
            pltpu.VMEM((components, points), jnp.bfloat16),
            pltpu.VMEM((rows, span, LANES), jnp.float32),
            like(sea_mask),
            like(depth_index),
            pltpu.SemaphoreType.DMA((14,)),
            pltpu.SemaphoreType.DMA((6,)),
        ]
        if last:
            shapes.append(block(2 * nfreq + 2 * TILE, LANES))
            more = [depths, group_speed, refraction]
            operands += more
            scratch += [like(shapes[2])] + [like(a) for a in more]
        return pl.pallas_call(
            functools.partial(source_kernel, chunk, freqs, last, comps),
            in_specs=[scalar] + [far] * len(operands),
            out_specs=[far] * len(shapes),
            out_shape=shapes,
            scratch_shapes=scratch,
            compiler_params=params(57 if chunk else 63),
            cost_estimate=cost(2 * span * components * points, 4 * components * points),
            name="source_terms",
        )(block_index, *operands)

    def coast(even, odd, kit):
        shapes = [
            block(rows + 5, nfreq, LANES),
            block(rows + 4, nfreq, LANES),
            block(nfreq // TILE, (rows + 4) * (ND // 2), TILE, LANES),
            block(rows + 4, TILE, LANES),
        ]
        return pl.pallas_call(
            functools.partial(coast_kernel, nfreq),
            in_specs=[scalar] + [near] * 3,
            out_specs=[near] * len(shapes),
            out_shape=shapes,
            scratch_shapes=[pltpu.VMEM((2 * (rows + 4), nfreq, LANES), jnp.float32)],
            compiler_params=params(24),
            cost_estimate=cost(ND * rows * nfreq * LANES, 4 * ND * rows * nfreq * LANES),
            name="coast_tables",
        )(block_index, even, odd, kit)

    def exchange(even, odd):
        odd = lax.ppermute(odd, BLOCKS, odd_swaps)
        return lax.ppermute(even, BLOCKS, even_swaps), odd

    work = pltpu.VMEM((freqs // TILE, rows, ND + 1, TILE, LANES), jnp.float32)

    passed = pltpu.VMEM((freqs // TILE, 4, rows, TILE, LANES), jnp.float32)

    trig = pltpu.SMEM((2, CLASSES), jnp.float32)

    def two_steps(chunk, state, halo, tables):
        operands = [block_index, *state, *halo, *tables]
        shapes = [tiles(ONE), tiles(ONE), tiles(ND)]
        return pl.pallas_call(
            functools.partial(two_steps_kernel, chunk, freqs),
            in_specs=[scalar] + [near] * (len(operands) - 1),
            out_specs=[near] * len(shapes),
            out_shape=shapes,
            scratch_shapes=[
                pltpu.VMEM((2, freqs // TILE, rows + 8, ND, TILE, LANES), jnp.float32),
                work,
                passed,
                trig,
            ],
            compiler_params=params(24),
            cost_estimate=cost(3 * 40 * span * points, 4 * 4 * span * points),
            name="two_substeps",
        )(*operands)

    def last_step(chunk, state, halo, tables, out):
        operands = [block_index, *state, *halo, *tables]
        specs = [scalar] + [near] * (len(operands) - 1)
        aliases = {}
        if out is not None:
            aliases = {len(operands): 0}
            operands.append(out)
            specs.append(far)
        return pl.pallas_call(
            functools.partial(last_step_kernel, chunk, freqs),
            in_specs=specs,
            out_specs=far,
            out_shape=block(*spectrum.shape),
            scratch_shapes=[
                pltpu.VMEM((freqs // TILE, rows + 4, ND, TILE, LANES), jnp.float32),
                work,
                passed,
                pltpu.VMEM((rows, span, LANES), jnp.float32),
                trig,
                pltpu.SemaphoreType.DMA((rows,)),
            ],
            input_output_aliases=aliases,
            compiler_params=params(24),
            cost_estimate=cost(40 * span * points, 4 * 4 * span * points),
            name="last_substep",
        )(*operands)

    states = []
    halos = []
    for chunk in range(CHUNKS):
        even, odd, *kit = source(chunk)
        states.append((even, odd))
        halos.append(exchange(even, odd))
    tables = coast(*halos[0], *kit)
    for chunk in range(CHUNKS):
        states[chunk] = two_steps(chunk, states[chunk], halos[chunk], tables)
        halos[chunk] = exchange(*states[chunk][:2])
    out = None
    for chunk in range(CHUNKS):
        out = last_step(chunk, states[chunk], halos[chunk], tables, out)
    return out


def solution(mesh):
    in_specs = (
        P(None, ("comp", "space")),
        P(None, ("comp", "space")),
        P(),
        P(),
        P(),
        P(),
        P(),
        P(),
        P("space", None),
        P("space", None),
    )
    out_specs = P(None, ("comp", "space"))
    return jax.shard_map(
        per_device, mesh=mesh, in_specs=in_specs, out_specs=out_specs, check_vma=False
    )
```

```python
import functools

import jax
import jax.numpy as jnp
import numpy as np
from jax import lax
from jax.experimental import pallas as pl
from jax.experimental.pallas import tpu as pltpu
from jax.sharding import PartitionSpec as P

ND = 36
LANES = 128
TILE = 8
CHUNKS = 2
WIDE_FIRST = (False, True)
BLOCKS = ("comp", "space")

ANGLES = 2.0 * np.pi * np.arange(ND) / ND
COS = [float(v) for v in np.cos(ANGLES)]
SIN = [float(v) for v in np.sin(ANGLES)]
HALF = 2.0 * np.pi * (np.arange(ND) + 0.5) / ND
SPREAD = float(np.cos(np.pi / ND))
COS_FACE = [float(v) * SPREAD for v in np.cos(HALF)]
SIN_FACE = [float(v) * SPREAD for v in np.sin(HALF)]

UPWARD = list(range(28, 36)) + list(range(0, 10))
DOWNWARD = list(range(10, 28))
CLASSES = 10

ONE = ND + 18
TWO = 2 * ND + 22 + 18
THIRD = 2 * ND
FOURTH = THIRD + 22


def places_one(row, d):
    up = d in UPWARD
    slot = (d + 8) % ND if up else d - 10
    if row == 3:
        return [(0, d)]
    if row == 0:
        return [(1, d)]
    if row == 2:
        return [(0, ND + slot)] if up else [(2, 18 + slot)]
    return [(2, slot)] if up else [(1, ND + slot)]


def places_two(row, d):
    up = d in UPWARD
    found = [(0, (3 - row) * ND + d)] if row >= 2 else [(1, row * ND + d)]
    if row == 1 and (d + 10) % ND < 22:
        found.append((0, THIRD + (d + 10) % ND))
    if row == 2 and 8 <= d < 30:
        found.append((1, THIRD + d - 8))
    if row == 0 and up:
        found.append((0, FOURTH + (d + 8) % ND))
    if row == 3 and not up:
        found.append((1, FOURTH + d - 10))
    return found


def pick_row(strip, row):
    index = lax.broadcasted_iota(jnp.int32, strip.shape, 0)
    return jnp.sum(jnp.where(index == row, strip, 0.0), axis=0, keepdims=True)


def column_of(row_values, first, count):
    size = row_values.shape[1]
    shape = (count, size)
    chosen = (
        lax.broadcasted_iota(jnp.int32, shape, 0) + first
        == lax.broadcasted_iota(jnp.int32, shape, 1)
    )
    return jnp.sum(jnp.where(chosen, row_values, 0.0), axis=1, keepdims=True)


def fetch(pairs, sems):
    copies = [pltpu.make_async_copy(src, dst, sems.at[i]) for i, (src, dst) in enumerate(pairs)]
    for copy in copies:
        copy.start()
    return copies


def run_copies(pairs, sems):
    for copy in fetch(pairs, sems):
        copy.wait()


def by_parity(odd, even_way, odd_way):
    pl.when(jnp.logical_not(odd))(even_way)
    pl.when(odd)(odd_way)


def source_kernel(chunk, freqs, wide, last, comps, *refs):
    refs = list(refs)
    rows = 4
    block = refs.pop(0)[0]
    spectrum, wind, coupling, growth_in, dissipation_in = (refs.pop(0) for _ in range(5))
    if last:
        coast_in = [refs.pop(0) for _ in range(5)]
    even_out, odd_out = refs.pop(0), refs.pop(0)
    if not wide:
        rest_out = refs.pop(0)
    if last:
        kit, edge = refs.pop(0), refs.pop(0)
    outs = [refs.pop(0) for _ in range(2 if wide else 3)]
    spec, wind_ref, operator, growth_ref, dissipation_ref, rounded, mixed = refs[:7]
    sems, out_sems = refs[7:9]
    span = freqs * ND
    pairs = [(spectrum.at[:, pl.ds(r * LANES, LANES)], spec.at[r]) for r in range(rows)]
    pairs += [
        (coupling.at[pl.ds(chunk * span, span), :], operator),
        (wind, wind_ref),
        (growth_in, growth_ref),
        (dissipation_in, dissipation_ref),
    ]
    if last:
        mask_ref, index_ref, depths_ref, speed_ref, refraction_ref = refs[9:]
        pairs += list(zip(coast_in, refs[9:]))
    copies = fetch(pairs, sems)
    for r in range(rows):
        copies[r].wait()
        rounded[:, r * LANES : (r + 1) * LANES] = spec[r].astype(jnp.bfloat16)
    for copy in copies[rows:]:
        copy.wait()
    nonlinear = jnp.dot(operator[...], rounded[...], preferred_element_type=jnp.float32)
    for r in range(rows):
        mixed[r] = nonlinear[:, r * LANES : (r + 1) * LANES]
    components = spec.shape[1]
    growth = column_of(growth_ref[...], chunk * freqs, freqs)
    dissipation = column_of(dissipation_ref[...], chunk * freqs, freqs)
    tiles = freqs // TILE
    odd = lax.rem(block, 2) == 1

    def leave(number, which, start, count):
        part = pl.ds(start, count)

        def begin(to):
            pltpu.make_async_copy(outs[which].at[part], to.at[part], out_sems.at[number]).start()

        by_parity(
            odd,
            lambda: begin((even_out, odd_out)[which]),
            lambda: begin((odd_out, even_out)[which]),
        )
        return pltpu.make_async_copy(outs[which].at[part], even_out.at[part], out_sems.at[number])

    for r in (3, 2, 1, 0):
        average = jnp.sum(spec[r], axis=0, keepdims=True) * (1.0 / components)
        limited = average / (average + 1.0)
        wind_x = jnp.broadcast_to(wind_ref[0:1, r * LANES : (r + 1) * LANES], (TILE, LANES))
        wind_y = jnp.broadcast_to(wind_ref[1:2, r * LANES : (r + 1) * LANES], (TILE, LANES))
        grow = []
        damp = []
        for t in range(tiles):
            part = slice(t * TILE, (t + 1) * TILE)
            grow.append(jnp.broadcast_to(growth[part], (TILE, LANES)))
            damp.append(dissipation[part] * limited)
        for d in range(ND):
            forcing = jnp.maximum(COS[d] * wind_x + SIN[d] * wind_y, 0.0)
            squared = forcing * forcing
            for t in range(tiles):
                base = (chunk * freqs + t * TILE) * ND + d
                energy = spec[r, pl.ds(base, TILE, stride=ND), :]
                extra = mixed[r, pl.ds(t * TILE * ND + d, TILE, stride=ND), :]
                value = energy + (grow[t] * squared - damp[t]) * energy + 0.25 * extra
                for which, slot in (places_two if wide else places_one)(r, d):
                    outs[which][slot, t * TILE : (t + 1) * TILE, :] = value
        if r == 2 and wide:
            leaving = [leave(0, 0, 0, THIRD), leave(1, 1, THIRD, TWO - THIRD)]
        elif r == 2:
            leaving = [leave(0, 0, 0, ONE)]
    if wide:
        leaving += [leave(2, 1, 0, THIRD), leave(3, 0, THIRD, TWO - THIRD)]
    else:
        rest_copy = pltpu.make_async_copy(outs[2], rest_out, out_sems.at[2])
        rest_copy.start()
        leaving += [leave(1, 1, 0, ONE), rest_copy]
    if last:
        first = lax.rem(block, comps) * rows
        mask = mask_ref[...].astype(jnp.float32)
        index = index_ref[...].astype(jnp.float32)
        count, levels = speed_ref.shape
        kit[...] = jnp.zeros_like(kit)
        kit[:count, :levels] = speed_ref[...]
        kit[count : 2 * count, :levels] = refraction_ref[...]
        kit[2 * count : 2 * count + 1, :levels] = depths_ref[...]
        for k in range(rows + 6):
            kit[2 * count + TILE + k, :] = pick_row(mask, first + k - 3)[0]
            kit[2 * count + 3 * TILE + k, :] = pick_row(index, first + k - 3)[0]
        near_side = first + jnp.where(odd, rows - 3, 0)
        edge[...] = jnp.zeros_like(edge)
        for k in range(3):
            edge[k, :] = pick_row(mask, near_side + k)[0]
            edge[3 + k, :] = pick_row(index, near_side + k)[0]
    for copy in leaving:
        copy.wait()


def weights(courant):
    half = 0.5 * courant
    square = courant * half
    curve = (half - courant * square) * (1.0 / 3.0)
    rising = half + square
    falling = half - square
    return rising + (curve + curve), falling - curve, curve


def coast_kernel(
    count, block_ref, far_ref, kit_ref, face_x, face_y, turn_ref, land_ref, slope_by
):
    rows = 4
    tables = kit_ref[: 2 * count + TILE, :]
    odd = (lax.rem(block_ref[0], 2) == 1).astype(jnp.float32)

    def with_far(start, part):
        found = [kit_ref[start + k : start + k + 1, :] for k in range(rows + 6)]
        for k in range(3):
            far = far_ref[part + k : part + k + 1, :]
            found[k] += far * (1.0 - odd)
            found[rows + 3 + k] += far * odd
        return found

    masks = with_far(2 * count + TILE, 0)
    levels = with_far(2 * count + 3 * TILE, 3)
    wanted = jnp.concatenate(levels, axis=1)
    entry = lax.broadcasted_iota(jnp.int32, (LANES, wanted.shape[1]), 0).astype(jnp.float32)
    onehot = (entry == wanted).astype(jnp.float32)
    looked = jnp.dot(
        tables, onehot, precision=lax.Precision.HIGHEST, preferred_element_type=jnp.float32
    )
    speeds = looked[:count]
    turns = looked[count : 2 * count]
    depth = looked[2 * count : 2 * count + 1]

    def at(values, i):
        return values[:, i * LANES : (i + 1) * LANES]

    heights = [at(depth, i) * masks[i] for i in range(rows + 6)]
    for face in range(rows + 5):
        weight = 0.5 * (masks[face] * masks[face + 1])
        face_x[face] = (at(speeds, face) + at(speeds, face + 1)) * weight
    lane = lax.broadcasted_iota(jnp.int32, (1, LANES), 1)
    for r in range(rows + 4):
        mask = masks[r + 1]
        after = jnp.where(lane < LANES - 1, pltpu.roll(mask, LANES - 1, 1), 0.0)
        speed = at(speeds, r + 1)
        face_y[r] = (speed + pltpu.roll(speed, LANES - 1, 1)) * (0.5 * (mask * after))
        slope_x = 0.5 * (heights[r + 2] - heights[r])
        height = heights[r + 1]
        next_height = jnp.where(lane < LANES - 1, pltpu.roll(height, LANES - 1, 1), 0.0)
        last_height = jnp.where(lane > 0, pltpu.roll(height, 1, 1), 0.0)
        slope_y = 0.5 * (next_height - last_height)
        turn = at(turns, r + 1)
        slope_by[2 * r] = turn * slope_x
        slope_by[2 * r + 1] = turn * slope_y
        land_ref[r] = jnp.broadcast_to(mask, (TILE, LANES))

    @pl.loop(0, count // TILE)
    def _(t):
        part = pl.ds(pl.multiple_of(t * TILE, TILE), TILE)

        @pl.loop(0, rows + 4)
        def _(r):
            turn_x = slope_by[2 * r, part, :]
            turn_y = slope_by[2 * r + 1, part, :]
            for d in range(ND // 2):
                turn_ref[t, r * (ND // 2) + d] = turn_x * SIN_FACE[d] - turn_y * COS_FACE[d]


def shift_rows_columns(
    part, first, last, cells_of, moved, x_ref, y_ref, base, trig, j, members, put
):
    along_x = {
        k: weights(x_ref[base + k, part, :] * trig[0, j]) for k in range(first, last + 2)
    }
    for i, (d, _, up, _) in enumerate(members):
        cell = functools.partial(cells_of, d)
        if up:
            cells = {r: cell(r) for r in range(first - 2, last + 2)}
            faces = {
                k: a * cells[k - 1] + b * cells[k] - c * cells[k - 2]
                for k, (a, b, c) in along_x.items()
            }
            for r in range(first, last + 1):
                moved[i, r - first] = cells[r] - (faces[r + 1] - faces[r])
        else:
            cells = {r: cell(r) for r in range(first - 1, last + 3)}
            faces = {
                k: a * cells[k] + b * cells[k - 1] - c * cells[k + 1]
                for k, (a, b, c) in along_x.items()
            }
            for r in range(first, last + 1):
                moved[i, r - first] = cells[r] + (faces[r + 1] - faces[r])
    lanes = lax.broadcasted_iota(jnp.int32, (TILE, LANES), 1)
    not_first = (lanes != 0).astype(jnp.float32)
    not_last = (lanes != LANES - 2).astype(jnp.float32)
    for r in range(first, last + 1):
        near, far, curve = weights(y_ref[base + r, part, :] * trig[1, j])
        curve_up = curve * not_first
        curve_down = curve * not_last
        for i, (_, d, _, to_higher) in enumerate(members):
            here = moved[i, r - first]
            after = pltpu.roll(here, LANES - 1, 1)
            if to_higher:
                before = pltpu.roll(here, 1, 1)
                face = near * here + far * after - curve_up * before
                result = here - (face - pltpu.roll(face, 1, 1))
            else:
                beyond = pltpu.roll(here, LANES - 2, 1)
                face = near * after + far * here - curve_down * beyond
                result = here + (face - pltpu.roll(face, 1, 1))
            put(r, d, result)


def every_class(tiles, one_class):
    @pl.loop(0, CLASSES)
    def _(j):
        single = jnp.logical_or(j == 0, j == 9)
        rising = jnp.where(j == 0, 0, ND - j)
        members = [
            (j, j, True, True),
            (rising, jnp.where(single, ND, rising), True, False),
            (18 - j, jnp.where(j == 9, ND, 18 - j), False, True),
            (18 + j, jnp.where(j == 0, ND, 18 + j), False, False),
        ]
        for t in range(tiles):
            one_class(t, j, members)


def turn_rows(jobs):
    half_turn = ND // 2

    def slope(read, i):
        return read((i + 1) % ND) - read(i % ND)

    def pair(read, turning, d, known):
        courant = turning(d)
        half = 0.5 * courant
        spread = (1.0 / 3.0) - courant * (courant * (1.0 / 3.0))
        positive = courant >= 0.0
        faces = []
        following = []
        for side in range(2):
            own = d + side * half_turn
            rise, bend = known[side]
            next_rise = slope(read, own + 1)
            next_bend = next_rise - rise
            total = read(own) + read((own + 1) % ND)
            if side == 0:
                chosen = jnp.where(positive, bend, next_bend)
                faces.append(half * ((total - courant * rise) - spread * chosen))
            else:
                chosen = jnp.where(positive, next_bend, bend)
                faces.append(half * ((total + courant * rise) - spread * chosen))
            following.append((next_rise, next_bend))
        return faces, following

    def known_at(read, d):
        found = []
        for side in range(2):
            own = d + side * half_turn
            rise = slope(read, own)
            found.append((rise, rise - slope(read, own - 1)))
        return found

    states = []
    for read, turning, _, _ in jobs:
        ends, following = pair(read, turning, half_turn - 1, known_at(read, half_turn - 1))
        states.append((ends, [0.0 - ends[1], 0.0 - ends[0]], [following[1], following[0]]))
    for d in range(half_turn):
        for i, (read, turning, land, put) in enumerate(jobs):
            ends, previous, known = states[i]
            if d == half_turn - 1:
                current = ends
            else:
                current, known = pair(read, turning, d, known)
            put(d, (read(d) - (current[0] - previous[0])) * land)
            own = d + half_turn
            put(own, (read(own) + (current[1] - previous[1])) * land)
            states[i] = (ends, current, known)


def set_trig(trig):
    for j in range(CLASSES):
        trig[0, j] = abs(COS[j])
        trig[1, j] = abs(SIN[j])


def output_row(packed, out_ref, start, span, r, sems):
    lanes = pl.ds(pl.multiple_of(r * LANES, LANES), LANES)
    return pltpu.make_async_copy(packed.at[r], out_ref.at[pl.ds(start, span), lanes], sems.at[r])


def two_steps_kernel(chunk, freqs, final, *refs):
    block_ref, even_own, odd_own, even_ref, odd_ref, x_ref, y_ref, turn_ref, land_ref = refs[:9]
    if final:
        out_ref, cells, work, moved, trig, packed, sems = refs[-7:]
    else:
        even_out, odd_out, rest_out, cells, work, moved, trig = refs[-7:]
    odd = lax.rem(block_ref[0], 2) == 1
    tiles = freqs // TILE
    half_turn = ND // 2
    set_trig(trig)
    parts = [slice(t * TILE, (t + 1) * TILE) for t in range(tiles)]

    def gather(up_ref, down_ref, low_ref, high_ref):
        @pl.loop(0, ND)
        def _(d):
            for t, part in enumerate(parts):
                for k in range(2):
                    cells[0, t, 3 - k, d] = low_ref[k * ND + d, part, :]
                    cells[0, t, 4 + k, d] = down_ref[k * ND + d, part, :]
                    cells[0, t, 7 - k, d] = up_ref[k * ND + d, part, :]
                    cells[0, t, 8 + k, d] = high_ref[k * ND + d, part, :]

        @pl.loop(0, 22)
        def _(i):
            for t, part in enumerate(parts):
                cells[0, t, 1, lax.rem(i + 26, ND)] = low_ref[THIRD + i, part, :]
                cells[0, t, 10, i + 8] = high_ref[THIRD + i, part, :]

        @pl.loop(0, 18)
        def _(i):
            for t, part in enumerate(parts):
                cells[0, t, 0, lax.rem(i + 28, ND)] = low_ref[FOURTH + i, part, :]
                cells[0, t, 11, i + 10] = high_ref[FOURTH + i, part, :]

    by_parity(
        odd,
        lambda: gather(even_own, odd_own, odd_ref, even_ref),
        lambda: gather(odd_own, even_own, even_ref, odd_ref),
    )

    @pl.loop(0, 3)
    def _(stage):
        source = stage // 2
        base = jnp.where(stage == 0, 2, jnp.where(stage == 1, 6, 4))

        def one_class(t, j, members):
            def cell(d, r):
                return cells[source, t, base + r, d]

            def put(r, d, value):
                work[t, r, d] = value

            table = pl.ds(chunk * freqs + t * TILE, TILE)
            shift_rows_columns(
                table, 0, 3, cell, moved.at[t], x_ref, y_ref, base - 2, trig, j, members, put
            )

        every_class(tiles, one_class)

        @pl.loop(0, tiles * 4)
        def _(i):
            t = i // 4
            r = lax.rem(i, 4)

            def put(d, value):
                cells[1 - source, t, base + r, d] = value

            turn_rows(
                [
                    (
                        lambda d: work[t, r, d],
                        lambda d: turn_ref[chunk * tiles + t, (base - 2 + r) * half_turn + d],
                        land_ref[base - 2 + r],
                        put,
                    )
                ]
            )

    if final:
        span = freqs * ND
        rows = 4

        @pl.loop(0, rows)
        def _(r):
            @pl.loop(0, ND)
            def _(d):
                for t in range(tiles):
                    place = pl.ds(t * (TILE * ND) + d, TILE, stride=ND)
                    packed[r, place, :] = cells[0, t, rows + r, d]

            output_row(packed, out_ref, chunk * span, span, r, sems).start()

        for r in range(rows):
            output_row(packed, out_ref, chunk * span, span, r, sems).wait()
        return

    def hand_out(up_out, down_out):
        @pl.loop(0, ND)
        def _(d):
            for t, part in enumerate(parts):
                up_out[d, part, :] = cells[0, t, 7, d]
                down_out[d, part, :] = cells[0, t, 4, d]

        @pl.loop(0, half_turn)
        def _(i):
            upward = lax.rem(i + 28, ND)
            for t, part in enumerate(parts):
                up_out[ND + i, part, :] = cells[0, t, 6, upward]
                down_out[ND + i, part, :] = cells[0, t, 5, i + 10]
                rest_out[i, part, :] = cells[0, t, 5, upward]
                rest_out[half_turn + i, part, :] = cells[0, t, 6, i + 10]

    by_parity(odd, lambda: hand_out(even_out, odd_out), lambda: hand_out(odd_out, even_out))


def one_step_kernel(chunk, freqs, final, *refs):
    refs = list(refs)
    odd = lax.rem(refs.pop(0)[0], 2) == 1
    even_own, odd_own, rest_ref, even_ref, odd_ref = (refs.pop(0) for _ in range(5))
    x_ref, y_ref, turn_ref, land_ref = (refs.pop(0) for _ in range(4))
    if final:
        out_ref, cells, work, moved, trig, packed, sems = refs[-7:]
    else:
        even_out, odd_out, cells, work, moved, trig = refs
    rows = 4
    tiles = freqs // TILE
    half_turn = ND // 2
    span = freqs * ND
    set_trig(trig)
    parts = [slice(t * TILE, (t + 1) * TILE) for t in range(tiles)]

    def gather(up_ref, down_ref, low_ref, high_ref):
        @pl.loop(0, ND)
        def _(d):
            for t, part in enumerate(parts):
                cells[t, 1, d] = low_ref[d, part, :]
                cells[t, 2, d] = down_ref[d, part, :]
                cells[t, 5, d] = up_ref[d, part, :]
                cells[t, 6, d] = high_ref[d, part, :]

        @pl.loop(0, half_turn)
        def _(i):
            upward = lax.rem(i + 28, ND)
            for t, part in enumerate(parts):
                cells[t, 0, upward] = low_ref[ND + i, part, :]
                cells[t, 3, upward] = rest_ref[i, part, :]
                cells[t, 4, upward] = up_ref[ND + i, part, :]
                cells[t, 3, i + 10] = down_ref[ND + i, part, :]
                cells[t, 4, i + 10] = rest_ref[half_turn + i, part, :]
                cells[t, 7, i + 10] = high_ref[ND + i, part, :]

    by_parity(
        odd,
        lambda: gather(even_own, odd_own, odd_ref, even_ref),
        lambda: gather(odd_own, even_own, even_ref, odd_ref),
    )

    def only_pass(t, j, members):
        def cell(d, r):
            return cells[t, r + 2, d]

        def put(r, d, value):
            work[t, r, d] = value

        table = pl.ds(chunk * freqs + t * TILE, TILE)
        shift_rows_columns(
            table, 0, 3, cell, moved.at[t], x_ref, y_ref, 2, trig, j, members, put
        )

    every_class(tiles, only_pass)

    @pl.loop(0, rows)
    def _(r):
        @pl.loop(0, tiles)
        def _(t):
            def put(d, value):
                if final:
                    packed[r, pl.ds(t * (TILE * ND) + d, TILE, stride=ND), :] = value
                else:
                    cells[t, r + 2, d] = value

            turn_rows(
                [
                    (
                        lambda d: work[t, r, d],
                        lambda d: turn_ref[chunk * tiles + t, (r + 2) * half_turn + d],
                        land_ref[r + 2],
                        put,
                    )
                ]
            )

        if final:
            output_row(packed, out_ref, chunk * span, span, r, sems).start()

    if final:
        for r in range(rows):
            output_row(packed, out_ref, chunk * span, span, r, sems).wait()
        return

    def hand_out(up_out, down_out):
        @pl.loop(0, ND)
        def _(d):
            for t, part in enumerate(parts):
                for k in range(2):
                    up_out[k * ND + d, part, :] = cells[t, 5 - k, d]
                    down_out[k * ND + d, part, :] = cells[t, 2 + k, d]

        @pl.loop(0, 22)
        def _(i):
            for t, part in enumerate(parts):
                up_out[THIRD + i, part, :] = cells[t, 3, lax.rem(i + 26, ND)]
                down_out[THIRD + i, part, :] = cells[t, 4, i + 8]

        @pl.loop(0, 18)
        def _(i):
            for t, part in enumerate(parts):
                up_out[FOURTH + i, part, :] = cells[t, 2, lax.rem(i + 28, ND)]
                down_out[FOURTH + i, part, :] = cells[t, 5, i + 10]

    by_parity(odd, lambda: hand_out(even_out, odd_out), lambda: hand_out(odd_out, even_out))


def cost(flops, size):
    return pl.CostEstimate(flops=flops, bytes_accessed=size, transcendentals=0)


def params(limit):
    return pltpu.CompilerParams(vmem_limit_bytes=limit * 1024 * 1024)


def per_device(
    spectrum,
    wind_field,
    coupling,
    growth,
    dissipation,
    group_speed,
    refraction,
    depths,
    sea_mask,
    depth_index,
):
    components, points = spectrum.shape
    nfreq = growth.shape[0]
    levels = depths.shape[0]
    rows = points // LANES
    freqs = nfreq // CHUNKS
    span = freqs * ND
    comps, strips = lax.axis_size("comp"), lax.axis_size("space")
    order = [c * strips + s for s in range(strips) for c in range(comps)]
    steps = list(zip(order[:-1], order[1:]))
    even_swaps = [swap for i, j in steps[0::2] for swap in ((i, j), (j, i))]
    odd_swaps = [swap for i, j in steps[1::2] for swap in ((i, j), (j, i))]
    strip_swaps = [swap for i, j in steps[comps - 1 :: comps] for swap in ((i, j), (j, i))]
    block_index = lax.axis_index("space") * comps + lax.axis_index("comp")
    block_index = block_index.astype(jnp.int32).reshape(1)
    scalar = pl.BlockSpec(memory_space=pltpu.SMEM)
    near = pl.BlockSpec(memory_space=pltpu.VMEM)
    far = pl.BlockSpec(memory_space=pltpu.HBM)
    growth = growth.reshape(1, nfreq)
    dissipation = dissipation.reshape(1, nfreq)
    depths = depths.reshape(1, levels)

    def block(*shape):
        return jax.ShapeDtypeStruct(shape, jnp.float32)

    def like(array):
        return pltpu.VMEM(array.shape, array.dtype)

    def tiles(count):
        return block(count, freqs, LANES)

    def source(chunk):
        last = chunk == CHUNKS - 1
        wide = WIDE_FIRST[chunk]
        shapes = [tiles(TWO)] * 2 if wide else [tiles(ONE), tiles(ONE), tiles(ND)]
        out_specs = [far] * len(shapes)
        operands = [spectrum, wind_field, coupling, growth, dissipation]
        scratch = [like(shape) for shape in shapes] + [
            pltpu.VMEM((rows, components, LANES), jnp.float32),
            like(wind_field),
            pltpu.VMEM((span, components), jnp.bfloat16),
            like(growth),
            like(dissipation),
            pltpu.VMEM((components, points), jnp.bfloat16),
            pltpu.VMEM((rows, span, LANES), jnp.float32),
            pltpu.SemaphoreType.DMA((13,)),
            pltpu.SemaphoreType.DMA((4,)),
        ]
        if last:
            shapes += [block(2 * nfreq + 5 * TILE, LANES), block(TILE, LANES)]
            out_specs += [near, near]
            more = [sea_mask, depth_index, depths, group_speed, refraction]
            operands += more
            scratch += [like(a) for a in more]
        return pl.pallas_call(
            functools.partial(source_kernel, chunk, freqs, wide, last, comps),
            in_specs=[scalar] + [far] * len(operands),
            out_specs=out_specs,
            out_shape=shapes,
            scratch_shapes=scratch,
            compiler_params=params(57 if chunk else 63),
            cost_estimate=cost(2 * span * components * points, 4 * components * points),
            name="source_terms",
        )(block_index, *operands)

    def coast(edge, kit):
        shapes = [
            block(rows + 5, nfreq, LANES),
            block(rows + 4, nfreq, LANES),
            block(nfreq // TILE, (rows + 4) * (ND // 2), TILE, LANES),
            block(rows + 4, TILE, LANES),
        ]
        return pl.pallas_call(
            functools.partial(coast_kernel, nfreq),
            in_specs=[scalar] + [near] * 2,
            out_specs=[near] * len(shapes),
            out_shape=shapes,
            scratch_shapes=[pltpu.VMEM((2 * (rows + 4), nfreq, LANES), jnp.float32)],
            compiler_params=params(24),
            cost_estimate=cost(ND * rows * nfreq * LANES, 4 * ND * rows * nfreq * LANES),
            name="coast_tables",
        )(block_index, edge, kit)

    def exchange(even, odd):
        odd = lax.ppermute(odd, BLOCKS, odd_swaps)
        return lax.ppermute(even, BLOCKS, even_swaps), odd

    work = pltpu.VMEM((freqs // TILE, rows, ND + 1, TILE, LANES), jnp.float32)

    passed = pltpu.VMEM((freqs // TILE, 4, rows, TILE, LANES), jnp.float32)

    trig = pltpu.SMEM((2, CLASSES), jnp.float32)

    def advance(kernel, name, chunk, state, halo, tables, shapes, buffers, out):
        operands = [block_index, *state, *halo, *tables]
        specs = [scalar] + [near] * (len(operands) - 1)
        scratch = [*buffers, work, passed, trig]
        aliases = {}
        final = not shapes
        if final:
            shapes = [block(*spectrum.shape)]
            scratch += [
                pltpu.VMEM((rows, span, LANES), jnp.float32),
                pltpu.SemaphoreType.DMA((rows,)),
            ]
            if out is not None:
                aliases = {len(operands): 0}
                operands.append(out)
                specs.append(far)
        return pl.pallas_call(
            functools.partial(kernel, chunk, freqs, final),
            in_specs=specs,
            out_specs=[far if final else near] * len(shapes),
            out_shape=shapes,
            scratch_shapes=scratch,
            input_output_aliases=aliases,
            compiler_params=params(24),
            cost_estimate=cost(2 * 40 * span * points, 4 * 4 * span * points),
            name=name,
        )(*operands)

    groups = freqs // TILE

    def two_steps(chunk, state, halo, tables, shapes=(), out=None):
        buffers = [pltpu.VMEM((2, groups, rows + 8, ND, TILE, LANES), jnp.float32)]
        name = "two_substeps"
        return advance(
            two_steps_kernel, name, chunk, state, halo, tables, shapes, buffers, out
        )

    def one_step(chunk, state, halo, tables, shapes=(), out=None):
        buffers = [pltpu.VMEM((groups, rows + 4, ND, TILE, LANES), jnp.float32)]
        name = "one_substep"
        return advance(
            one_step_kernel, name, chunk, state, halo, tables, shapes, buffers, out
        )

    narrow = [tiles(ONE), tiles(ONE), tiles(ND)]
    states = []
    halos = []
    for chunk in range(CHUNKS):
        even, odd, *more = source(chunk)
        states.append((even, odd) if WIDE_FIRST[chunk] else (even, odd, more[0]))
        halos.append(exchange(even, odd))
    kit, edge = more[-2:]
    tables = coast(lax.ppermute(edge, BLOCKS, strip_swaps), kit)
    for chunk in range(CHUNKS):
        if WIDE_FIRST[chunk]:
            made = two_steps(chunk, states[chunk], halos[chunk], tables, narrow)
        else:
            made = one_step(chunk, states[chunk], halos[chunk], tables, [tiles(TWO)] * 2)
        states[chunk] = made
        halos[chunk] = exchange(*made[:2])
    out = None
    for chunk in range(CHUNKS):
        step = one_step if WIDE_FIRST[chunk] else two_steps
        (out,) = step(chunk, states[chunk], halos[chunk], tables, out=out)
    return out


def solution(mesh):
    in_specs = (
        P(None, ("comp", "space")),
        P(None, ("comp", "space")),
        P(),
        P(),
        P(),
        P(),
        P(),
        P(),
        P("space", None),
        P("space", None),
    )
    out_specs = P(None, ("comp", "space"))
    return jax.shard_map(
        per_device, mesh=mesh, in_specs=in_specs, out_specs=out_specs, check_vma=False
    )
```

```python
import functools

import jax
import jax.numpy as jnp
import numpy as np
from jax import lax
from jax.experimental import pallas as pl
from jax.experimental.pallas import tpu as pltpu
from jax.sharding import PartitionSpec as P

ND = 36
LANES = 128
TILE = 8
CHUNKS = 2
WIDE_FIRST = (False, True)
BLOCKS = ("comp", "space")

ANGLES = 2.0 * np.pi * np.arange(ND) / ND
COS = [float(v) for v in np.cos(ANGLES)]
SIN = [float(v) for v in np.sin(ANGLES)]
HALF = 2.0 * np.pi * (np.arange(ND) + 0.5) / ND
SPREAD = float(np.cos(np.pi / ND))
COS_FACE = [float(v) * SPREAD for v in np.cos(HALF)]
SIN_FACE = [float(v) * SPREAD for v in np.sin(HALF)]

UPWARD = list(range(28, 36)) + list(range(0, 10))
DOWNWARD = list(range(10, 28))
CLASSES = 10

ONE = ND + 18
TWO = 2 * ND + 22 + 18
THIRD = 2 * ND
FOURTH = THIRD + 22


def places_one(row, d):
    up = d in UPWARD
    slot = (d + 8) % ND if up else d - 10
    if row == 3:
        return [(0, d)]
    if row == 0:
        return [(1, d)]
    if row == 2:
        return [(0, ND + slot)] if up else [(2, 18 + slot)]
    return [(2, slot)] if up else [(1, ND + slot)]


def places_two(row, d):
    up = d in UPWARD
    found = [(0, (3 - row) * ND + d)] if row >= 2 else [(1, row * ND + d)]
    if row == 1 and (d + 10) % ND < 22:
        found.append((0, THIRD + (d + 10) % ND))
    if row == 2 and 8 <= d < 30:
        found.append((1, THIRD + d - 8))
    if row == 0 and up:
        found.append((0, FOURTH + (d + 8) % ND))
    if row == 3 and not up:
        found.append((1, FOURTH + d - 10))
    return found


def pick_row(strip, row):
    index = lax.broadcasted_iota(jnp.int32, strip.shape, 0)
    return jnp.sum(jnp.where(index == row, strip, 0.0), axis=0, keepdims=True)


def column_of(row_values, first, count):
    size = row_values.shape[1]
    shape = (count, size)
    chosen = (
        lax.broadcasted_iota(jnp.int32, shape, 0) + first
        == lax.broadcasted_iota(jnp.int32, shape, 1)
    )
    return jnp.sum(jnp.where(chosen, row_values, 0.0), axis=1, keepdims=True)


def fetch(pairs, sems):
    copies = [pltpu.make_async_copy(src, dst, sems.at[i]) for i, (src, dst) in enumerate(pairs)]
    for copy in copies:
        copy.start()
    return copies


def run_copies(pairs, sems):
    for copy in fetch(pairs, sems):
        copy.wait()


def by_parity(odd, even_way, odd_way):
    pl.when(jnp.logical_not(odd))(even_way)
    pl.when(odd)(odd_way)


def source_kernel(chunk, freqs, wide, last, comps, *refs):
    refs = list(refs)
    rows = 4
    block = refs.pop(0)[0]
    spectrum, wind, coupling, growth_in, dissipation_in, mask_in, index_in = (
        refs.pop(0) for _ in range(7)
    )
    if last:
        tables_in = [refs.pop(0) for _ in range(3)]
    even_out, odd_out = refs.pop(0), refs.pop(0)
    if not wide:
        rest_out = refs.pop(0)
    if last:
        kit = refs.pop(0)
    outs = [refs.pop(0) for _ in range(2 if wide else 3)]
    spec, wind_ref, operator, growth_ref, dissipation_ref, rounded, mixed = refs[:7]
    mask_ref, index_ref, sems, out_sems = refs[7:11]
    span = freqs * ND
    pairs = [(spectrum.at[:, pl.ds(r * LANES, LANES)], spec.at[r]) for r in range(rows)]
    pairs += [
        (coupling.at[pl.ds(chunk * span, span), :], operator),
        (wind, wind_ref),
        (growth_in, growth_ref),
        (dissipation_in, dissipation_ref),
        (mask_in, mask_ref),
        (index_in, index_ref),
    ]
    if last:
        depths_ref, speed_ref, refraction_ref = refs[11:]
        pairs += list(zip(tables_in, refs[11:]))
    copies = fetch(pairs, sems)
    for r in range(rows):
        copies[r].wait()
        rounded[:, r * LANES : (r + 1) * LANES] = spec[r].astype(jnp.bfloat16)
    for copy in copies[rows:]:
        copy.wait()
    nonlinear = jnp.dot(operator[...], rounded[...], preferred_element_type=jnp.float32)
    for r in range(rows):
        mixed[r] = nonlinear[:, r * LANES : (r + 1) * LANES]
    components = spec.shape[1]
    growth = column_of(growth_ref[...], chunk * freqs, freqs)
    dissipation = column_of(dissipation_ref[...], chunk * freqs, freqs)
    tiles = freqs // TILE
    odd = lax.rem(block, 2) == 1

    def leave(number, which, start, count):
        part = pl.ds(start, count)

        def begin(to):
            pltpu.make_async_copy(outs[which].at[part], to.at[part], out_sems.at[number]).start()

        by_parity(
            odd,
            lambda: begin((even_out, odd_out)[which]),
            lambda: begin((odd_out, even_out)[which]),
        )
        return pltpu.make_async_copy(outs[which].at[part], even_out.at[part], out_sems.at[number])

    first = lax.rem(block, comps) * rows
    mask = mask_ref[...].astype(jnp.float32)
    index = index_ref[...].astype(jnp.float32)
    if not wide:
        near_side = first + jnp.where(odd, rows - 3, 0)
        edge = [pick_row(strip, near_side + k) for strip in (mask, index) for k in range(3)]
        edge = jnp.concatenate(edge + [jnp.zeros((freqs - 6, LANES), jnp.float32)], axis=0)
        outs[0][ONE] = edge
        outs[1][ONE] = edge
    for r in (3, 2, 1, 0):
        average = jnp.sum(spec[r], axis=0, keepdims=True) * (1.0 / components)
        limited = average / (average + 1.0)
        wind_x = jnp.broadcast_to(wind_ref[0:1, r * LANES : (r + 1) * LANES], (TILE, LANES))
        wind_y = jnp.broadcast_to(wind_ref[1:2, r * LANES : (r + 1) * LANES], (TILE, LANES))
        grow = []
        damp = []
        for t in range(tiles):
            part = slice(t * TILE, (t + 1) * TILE)
            grow.append(jnp.broadcast_to(growth[part], (TILE, LANES)))
            damp.append(dissipation[part] * limited)
        for d in range(ND):
            forcing = jnp.maximum(COS[d] * wind_x + SIN[d] * wind_y, 0.0)
            squared = forcing * forcing
            for t in range(tiles):
                base = (chunk * freqs + t * TILE) * ND + d
                energy = spec[r, pl.ds(base, TILE, stride=ND), :]
                extra = mixed[r, pl.ds(t * TILE * ND + d, TILE, stride=ND), :]
                value = energy + (grow[t] * squared - damp[t]) * energy + 0.25 * extra
                for which, slot in (places_two if wide else places_one)(r, d):
                    outs[which][slot, t * TILE : (t + 1) * TILE, :] = value
        if r == 2 and wide:
            leaving = [leave(0, 0, 0, THIRD), leave(1, 1, THIRD, TWO - THIRD)]
        elif r == 2:
            leaving = [leave(0, 0, 0, ONE + 1)]
    if wide:
        leaving += [leave(2, 1, 0, THIRD), leave(3, 0, THIRD, TWO - THIRD)]
    else:
        rest_copy = pltpu.make_async_copy(outs[2], rest_out, out_sems.at[2])
        rest_copy.start()
        leaving += [leave(1, 1, 0, ONE + 1), rest_copy]
    if last:
        count, levels = speed_ref.shape
        kit[...] = jnp.zeros_like(kit)
        kit[:count, :levels] = speed_ref[...]
        kit[count : 2 * count, :levels] = refraction_ref[...]
        kit[2 * count : 2 * count + 1, :levels] = depths_ref[...]
        for k in range(rows + 6):
            kit[2 * count + TILE + k, :] = pick_row(mask, first + k - 3)[0]
            kit[2 * count + 3 * TILE + k, :] = pick_row(index, first + k - 3)[0]
    for copy in leaving:
        copy.wait()


def weights(courant):
    half = 0.5 * courant
    square = courant * half
    curve = (half - courant * square) * (1.0 / 3.0)
    rising = half + square
    falling = half - square
    return rising + (curve + curve), falling - curve, curve


def coast_kernel(
    count, comps, block_ref, far_ref, kit_ref, face_x, face_y, turn_ref, land_ref, slope_by
):
    rows = 4
    tables = kit_ref[: 2 * count + TILE, :]
    place = lax.rem(block_ref[0], comps)
    below = (place == 0).astype(jnp.float32)
    above = (place == comps - 1).astype(jnp.float32)

    def with_far(start, part):
        found = [kit_ref[start + k : start + k + 1, :] for k in range(rows + 6)]
        for k in range(3):
            far = far_ref[ONE, part + k : part + k + 1, :]
            found[k] += far * below
            found[rows + 3 + k] += far * above
        return found

    masks = with_far(2 * count + TILE, 0)
    levels = with_far(2 * count + 3 * TILE, 3)
    wanted = jnp.concatenate(levels, axis=1)
    entry = lax.broadcasted_iota(jnp.int32, (LANES, wanted.shape[1]), 0).astype(jnp.float32)
    onehot = (entry == wanted).astype(jnp.float32)
    looked = jnp.dot(
        tables, onehot, precision=lax.Precision.HIGHEST, preferred_element_type=jnp.float32
    )
    speeds = looked[:count]
    turns = looked[count : 2 * count]
    depth = looked[2 * count : 2 * count + 1]

    def at(values, i):
        return values[:, i * LANES : (i + 1) * LANES]

    heights = [at(depth, i) * masks[i] for i in range(rows + 6)]
    for face in range(rows + 5):
        weight = 0.5 * (masks[face] * masks[face + 1])
        face_x[face] = (at(speeds, face) + at(speeds, face + 1)) * weight
    lane = lax.broadcasted_iota(jnp.int32, (1, LANES), 1)
    for r in range(rows + 4):
        mask = masks[r + 1]
        after = jnp.where(lane < LANES - 1, pltpu.roll(mask, LANES - 1, 1), 0.0)
        speed = at(speeds, r + 1)
        face_y[r] = (speed + pltpu.roll(speed, LANES - 1, 1)) * (0.5 * (mask * after))
        slope_x = 0.5 * (heights[r + 2] - heights[r])
        height = heights[r + 1]
        next_height = jnp.where(lane < LANES - 1, pltpu.roll(height, LANES - 1, 1), 0.0)
        last_height = jnp.where(lane > 0, pltpu.roll(height, 1, 1), 0.0)
        slope_y = 0.5 * (next_height - last_height)
        turn = at(turns, r + 1)
        slope_by[2 * r] = turn * slope_x
        slope_by[2 * r + 1] = turn * slope_y
        land_ref[r] = jnp.broadcast_to(mask, (TILE, LANES))

    @pl.loop(0, count // TILE)
    def _(t):
        part = pl.ds(pl.multiple_of(t * TILE, TILE), TILE)

        @pl.loop(0, rows + 4)
        def _(r):
            turn_x = slope_by[2 * r, part, :]
            turn_y = slope_by[2 * r + 1, part, :]
            for d in range(ND // 2):
                turn_ref[t, r * (ND // 2) + d] = turn_x * SIN_FACE[d] - turn_y * COS_FACE[d]


def shift_rows_columns(
    part, first, last, cells_of, moved, x_ref, y_ref, base, trig, j, members, put
):
    along_x = {
        k: weights(x_ref[base + k, part, :] * trig[0, j]) for k in range(first, last + 2)
    }
    for i, (d, _, up, _) in enumerate(members):
        cell = functools.partial(cells_of, d)
        if up:
            cells = {r: cell(r) for r in range(first - 2, last + 2)}
            faces = {
                k: a * cells[k - 1] + b * cells[k] - c * cells[k - 2]
                for k, (a, b, c) in along_x.items()
            }
            for r in range(first, last + 1):
                moved[i, r - first] = cells[r] - (faces[r + 1] - faces[r])
        else:
            cells = {r: cell(r) for r in range(first - 1, last + 3)}
            faces = {
                k: a * cells[k] + b * cells[k - 1] - c * cells[k + 1]
                for k, (a, b, c) in along_x.items()
            }
            for r in range(first, last + 1):
                moved[i, r - first] = cells[r] + (faces[r + 1] - faces[r])
    lanes = lax.broadcasted_iota(jnp.int32, (TILE, LANES), 1)
    not_first = (lanes != 0).astype(jnp.float32)
    not_last = (lanes != LANES - 2).astype(jnp.float32)
    for r in range(first, last + 1):
        near, far, curve = weights(y_ref[base + r, part, :] * trig[1, j])
        curve_up = curve * not_first
        curve_down = curve * not_last
        for i, (_, d, _, to_higher) in enumerate(members):
            here = moved[i, r - first]
            after = pltpu.roll(here, LANES - 1, 1)
            if to_higher:
                before = pltpu.roll(here, 1, 1)
                face = near * here + far * after - curve_up * before
                result = here - (face - pltpu.roll(face, 1, 1))
            else:
                beyond = pltpu.roll(here, LANES - 2, 1)
                face = near * after + far * here - curve_down * beyond
                result = here + (face - pltpu.roll(face, 1, 1))
            put(r, d, result)


def every_class(tiles, one_class):
    @pl.loop(0, CLASSES)
    def _(j):
        single = jnp.logical_or(j == 0, j == 9)
        rising = jnp.where(j == 0, 0, ND - j)
        members = [
            (j, j, True, True),
            (rising, jnp.where(single, ND, rising), True, False),
            (18 - j, jnp.where(j == 9, ND, 18 - j), False, True),
            (18 + j, jnp.where(j == 0, ND, 18 + j), False, False),
        ]
        for t in range(tiles):
            one_class(t, j, members)


def turn_rows(jobs):
    half_turn = ND // 2

    def slope(read, i):
        return read((i + 1) % ND) - read(i % ND)

    def pair(read, turning, d, known):
        courant = turning(d)
        half = 0.5 * courant
        spread = (1.0 / 3.0) - courant * (courant * (1.0 / 3.0))
        positive = courant >= 0.0
        faces = []
        following = []
        for side in range(2):
            own = d + side * half_turn
            rise, bend = known[side]
            next_rise = slope(read, own + 1)
            next_bend = next_rise - rise
            total = read(own) + read((own + 1) % ND)
            if side == 0:
                chosen = jnp.where(positive, bend, next_bend)
                faces.append(half * ((total - courant * rise) - spread * chosen))
            else:
                chosen = jnp.where(positive, next_bend, bend)
                faces.append(half * ((total + courant * rise) - spread * chosen))
            following.append((next_rise, next_bend))
        return faces, following

    def known_at(read, d):
        found = []
        for side in range(2):
            own = d + side * half_turn
            rise = slope(read, own)
            found.append((rise, rise - slope(read, own - 1)))
        return found

    states = []
    for read, turning, _, _ in jobs:
        ends, following = pair(read, turning, half_turn - 1, known_at(read, half_turn - 1))
        states.append((ends, [0.0 - ends[1], 0.0 - ends[0]], [following[1], following[0]]))
    for d in range(half_turn):
        for i, (read, turning, land, put) in enumerate(jobs):
            ends, previous, known = states[i]
            if d == half_turn - 1:
                current = ends
            else:
                current, known = pair(read, turning, d, known)
            put(d, (read(d) - (current[0] - previous[0])) * land)
            own = d + half_turn
            put(own, (read(own) + (current[1] - previous[1])) * land)
            states[i] = (ends, current, known)


def set_trig(trig):
    for j in range(CLASSES):
        trig[0, j] = abs(COS[j])
        trig[1, j] = abs(SIN[j])


def output_row(packed, out_ref, start, span, r, sems):
    lanes = pl.ds(pl.multiple_of(r * LANES, LANES), LANES)
    return pltpu.make_async_copy(packed.at[r], out_ref.at[pl.ds(start, span), lanes], sems.at[r])


def two_steps_kernel(chunk, freqs, final, *refs):
    block_ref, even_own, odd_own, *halo = refs[: 5 if final else 6]
    x_ref, y_ref, turn_ref, land_ref = refs[3 + len(halo) : 7 + len(halo)]
    if final:
        out_ref, cells, work, moved, trig, packed, sems = refs[-7:]
    else:
        even_out, odd_out, rest_out, cells, work, moved, trig = refs[-7:]
    odd = lax.rem(block_ref[0], 2) == 1
    tiles = freqs // TILE
    half_turn = ND // 2
    set_trig(trig)
    parts = [slice(t * TILE, (t + 1) * TILE) for t in range(tiles)]

    def gather(up_ref, down_ref, low_ref, high_ref):
        @pl.loop(0, ND, unroll=4)
        def _(d):
            for t, part in enumerate(parts):
                for k in range(2):
                    cells[0, t, 3 - k, d] = low_ref[k * ND + d, part, :]
                    cells[0, t, 4 + k, d] = down_ref[k * ND + d, part, :]
                    cells[0, t, 7 - k, d] = up_ref[k * ND + d, part, :]
                    cells[0, t, 8 + k, d] = high_ref[k * ND + d, part, :]

        @pl.loop(0, 22, unroll=11)
        def _(i):
            for t, part in enumerate(parts):
                cells[0, t, 1, lax.rem(i + 26, ND)] = low_ref[THIRD + i, part, :]
                cells[0, t, 10, i + 8] = high_ref[THIRD + i, part, :]

        @pl.loop(0, 18, unroll=9)
        def _(i):
            for t, part in enumerate(parts):
                cells[0, t, 0, lax.rem(i + 28, ND)] = low_ref[FOURTH + i, part, :]
                cells[0, t, 11, i + 10] = high_ref[FOURTH + i, part, :]

    even_ref, *odds = halo
    for place in range(4):
        odd_ref = odds[0] if place in (1, 2) else odds[-1]
        low, high = (even_ref, odd_ref) if place % 2 else (odd_ref, even_ref)
        own = (odd_own, even_own) if place % 2 else (even_own, odd_own)
        pl.when(lax.rem(block_ref[0], 4) == place)(functools.partial(gather, *own, low, high))

    @pl.loop(0, 3)
    def _(stage):
        source = stage // 2
        base = jnp.where(stage == 0, 2, jnp.where(stage == 1, 6, 4))

        def one_class(t, j, members):
            def cell(d, r):
                return cells[source, t, base + r, d]

            def put(r, d, value):
                work[t, r, d] = value

            table = pl.ds(chunk * freqs + t * TILE, TILE)
            shift_rows_columns(
                table, 0, 3, cell, moved.at[t], x_ref, y_ref, base - 2, trig, j, members, put
            )

        every_class(tiles, one_class)

        @pl.loop(0, tiles * 4)
        def _(i):
            t = i // 4
            r = lax.rem(i, 4)

            def put(d, value):
                cells[1 - source, t, base + r, d] = value

            turn_rows(
                [
                    (
                        lambda d: work[t, r, d],
                        lambda d: turn_ref[chunk * tiles + t, (base - 2 + r) * half_turn + d],
                        land_ref[base - 2 + r],
                        put,
                    )
                ]
            )

    if final:
        span = freqs * ND
        rows = 4

        @pl.loop(0, rows)
        def _(r):
            @pl.loop(0, ND, unroll=6)
            def _(d):
                for t in range(tiles):
                    place = pl.ds(t * (TILE * ND) + d, TILE, stride=ND)
                    packed[r, place, :] = cells[0, t, rows + r, d]

            output_row(packed, out_ref, chunk * span, span, r, sems).start()

        for r in range(rows):
            output_row(packed, out_ref, chunk * span, span, r, sems).wait()
        return

    def hand_out(up_out, down_out):
        @pl.loop(0, ND, unroll=4)
        def _(d):
            for t, part in enumerate(parts):
                up_out[d, part, :] = cells[0, t, 7, d]
                down_out[d, part, :] = cells[0, t, 4, d]

        @pl.loop(0, half_turn, unroll=6)
        def _(i):
            upward = lax.rem(i + 28, ND)
            for t, part in enumerate(parts):
                up_out[ND + i, part, :] = cells[0, t, 6, upward]
                down_out[ND + i, part, :] = cells[0, t, 5, i + 10]
                rest_out[i, part, :] = cells[0, t, 5, upward]
                rest_out[half_turn + i, part, :] = cells[0, t, 6, i + 10]

    by_parity(odd, lambda: hand_out(even_out, odd_out), lambda: hand_out(odd_out, even_out))


def one_step_kernel(chunk, freqs, final, *refs):
    refs = list(refs)
    odd = lax.rem(refs.pop(0)[0], 2) == 1
    even_own, odd_own, rest_ref, even_ref, odd_ref = (refs.pop(0) for _ in range(5))
    x_ref, y_ref, turn_ref, land_ref = (refs.pop(0) for _ in range(4))
    if final:
        out_ref, cells, work, moved, trig, packed, sems = refs[-7:]
    else:
        even_out, odd_out, cells, work, moved, trig = refs
    rows = 4
    tiles = freqs // TILE
    half_turn = ND // 2
    span = freqs * ND
    set_trig(trig)
    parts = [slice(t * TILE, (t + 1) * TILE) for t in range(tiles)]

    def gather(up_ref, down_ref, low_ref, high_ref):
        @pl.loop(0, ND, unroll=4)
        def _(d):
            for t, part in enumerate(parts):
                cells[t, 1, d] = low_ref[d, part, :]
                cells[t, 2, d] = down_ref[d, part, :]
                cells[t, 5, d] = up_ref[d, part, :]
                cells[t, 6, d] = high_ref[d, part, :]

        @pl.loop(0, half_turn, unroll=6)
        def _(i):
            upward = lax.rem(i + 28, ND)
            for t, part in enumerate(parts):
                cells[t, 0, upward] = low_ref[ND + i, part, :]
                cells[t, 3, upward] = rest_ref[i, part, :]
                cells[t, 4, upward] = up_ref[ND + i, part, :]
                cells[t, 3, i + 10] = down_ref[ND + i, part, :]
                cells[t, 4, i + 10] = rest_ref[half_turn + i, part, :]
                cells[t, 7, i + 10] = high_ref[ND + i, part, :]

    by_parity(
        odd,
        lambda: gather(even_own, odd_own, odd_ref, even_ref),
        lambda: gather(odd_own, even_own, even_ref, odd_ref),
    )

    def only_pass(t, j, members):
        def cell(d, r):
            return cells[t, r + 2, d]

        def put(r, d, value):
            work[t, r, d] = value

        table = pl.ds(chunk * freqs + t * TILE, TILE)
        shift_rows_columns(
            table, 0, 3, cell, moved.at[t], x_ref, y_ref, 2, trig, j, members, put
        )

    every_class(tiles, only_pass)

    @pl.loop(0, rows)
    def _(r):
        @pl.loop(0, tiles)
        def _(t):
            def put(d, value):
                if final:
                    packed[r, pl.ds(t * (TILE * ND) + d, TILE, stride=ND), :] = value
                else:
                    cells[t, r + 2, d] = value

            turn_rows(
                [
                    (
                        lambda d: work[t, r, d],
                        lambda d: turn_ref[chunk * tiles + t, (r + 2) * half_turn + d],
                        land_ref[r + 2],
                        put,
                    )
                ]
            )

        if final:
            output_row(packed, out_ref, chunk * span, span, r, sems).start()

    if final:
        for r in range(rows):
            output_row(packed, out_ref, chunk * span, span, r, sems).wait()
        return

    def hand_out(up_out, down_out):
        @pl.loop(0, ND, unroll=4)
        def _(d):
            for t, part in enumerate(parts):
                for k in range(2):
                    up_out[k * ND + d, part, :] = cells[t, 5 - k, d]
                    down_out[k * ND + d, part, :] = cells[t, 2 + k, d]

        @pl.loop(0, 22, unroll=11)
        def _(i):
            for t, part in enumerate(parts):
                up_out[THIRD + i, part, :] = cells[t, 3, lax.rem(i + 26, ND)]
                down_out[THIRD + i, part, :] = cells[t, 4, i + 8]

        @pl.loop(0, 18, unroll=9)
        def _(i):
            for t, part in enumerate(parts):
                up_out[FOURTH + i, part, :] = cells[t, 2, lax.rem(i + 28, ND)]
                down_out[FOURTH + i, part, :] = cells[t, 5, i + 10]

    by_parity(odd, lambda: hand_out(even_out, odd_out), lambda: hand_out(odd_out, even_out))


def cost(flops, size):
    return pl.CostEstimate(flops=flops, bytes_accessed=size, transcendentals=0)


def params(limit):
    return pltpu.CompilerParams(vmem_limit_bytes=limit * 1024 * 1024)


def per_device(
    spectrum,
    wind_field,
    coupling,
    growth,
    dissipation,
    group_speed,
    refraction,
    depths,
    sea_mask,
    depth_index,
):
    components, points = spectrum.shape
    nfreq = growth.shape[0]
    levels = depths.shape[0]
    rows = points // LANES
    freqs = nfreq // CHUNKS
    span = freqs * ND
    comps, strips = lax.axis_size("comp"), lax.axis_size("space")
    order = [c * strips + s for s in range(strips) for c in range(comps)]
    steps = list(zip(order[:-1], order[1:]))
    even_swaps = [swap for i, j in steps[0::2] for swap in ((i, j), (j, i))]
    odd_swaps = [swap for i, j in steps[1::2] for swap in ((i, j), (j, i))]
    block_index = lax.axis_index("space") * comps + lax.axis_index("comp")
    block_index = block_index.astype(jnp.int32).reshape(1)
    scalar = pl.BlockSpec(memory_space=pltpu.SMEM)
    near = pl.BlockSpec(memory_space=pltpu.VMEM)
    far = pl.BlockSpec(memory_space=pltpu.HBM)
    growth = growth.reshape(1, nfreq)
    dissipation = dissipation.reshape(1, nfreq)
    depths = depths.reshape(1, levels)

    def block(*shape):
        return jax.ShapeDtypeStruct(shape, jnp.float32)

    def like(array):
        return pltpu.VMEM(array.shape, array.dtype)

    def tiles(count):
        return block(count, freqs, LANES)

    def source(chunk):
        last = chunk == CHUNKS - 1
        wide = WIDE_FIRST[chunk]
        shapes = [tiles(TWO)] * 2 if wide else [tiles(ONE + 1), tiles(ONE + 1), tiles(ND)]
        out_specs = [far] * len(shapes)
        operands = [spectrum, wind_field, coupling, growth, dissipation, sea_mask, depth_index]
        scratch = [like(shape) for shape in shapes] + [
            pltpu.VMEM((rows, components, LANES), jnp.float32),
            like(wind_field),
            pltpu.VMEM((span, components), jnp.bfloat16),
            like(growth),
            like(dissipation),
            pltpu.VMEM((components, points), jnp.bfloat16),
            pltpu.VMEM((rows, span, LANES), jnp.float32),
            like(sea_mask),
            like(depth_index),
            pltpu.SemaphoreType.DMA((13,)),
            pltpu.SemaphoreType.DMA((4,)),
        ]
        if last:
            shapes += [block(2 * nfreq + 5 * TILE, LANES)]
            out_specs += [near]
            more = [depths, group_speed, refraction]
            operands += more
            scratch += [like(a) for a in more]
        return pl.pallas_call(
            functools.partial(source_kernel, chunk, freqs, wide, last, comps),
            in_specs=[scalar] + [far] * len(operands),
            out_specs=out_specs,
            out_shape=shapes,
            scratch_shapes=scratch,
            compiler_params=params(57 if chunk else 63),
            cost_estimate=cost(2 * span * components * points, 4 * components * points),
            name="source_terms",
        )(block_index, *operands)

    def coast(edge, kit):
        shapes = [
            block(rows + 5, nfreq, LANES),
            block(rows + 4, nfreq, LANES),
            block(nfreq // TILE, (rows + 4) * (ND // 2), TILE, LANES),
            block(rows + 4, TILE, LANES),
        ]
        return pl.pallas_call(
            functools.partial(coast_kernel, nfreq, comps),
            in_specs=[scalar] + [near] * 2,
            out_specs=[near] * len(shapes),
            out_shape=shapes,
            scratch_shapes=[pltpu.VMEM((2 * (rows + 4), nfreq, LANES), jnp.float32)],
            compiler_params=params(24),
            cost_estimate=cost(ND * rows * nfreq * LANES, 4 * ND * rows * nfreq * LANES),
            name="coast_tables",
        )(block_index, edge, kit)

    def exchange(even, odd):
        odd = lax.ppermute(odd, BLOCKS, odd_swaps)
        return lax.ppermute(even, BLOCKS, even_swaps), odd

    first_swaps = [swap for i, j in steps[1::4] for swap in ((i, j), (j, i))]
    later_swaps = [swap for i, j in steps[3::4] for swap in ((i, j), (j, i))]

    work = pltpu.VMEM((freqs // TILE, rows, ND + 1, TILE, LANES), jnp.float32)

    passed = pltpu.VMEM((freqs // TILE, 4, rows, TILE, LANES), jnp.float32)

    trig = pltpu.SMEM((2, CLASSES), jnp.float32)

    def advance(kernel, name, chunk, state, halo, tables, shapes, buffers, out):
        operands = [block_index, *state, *halo, *tables]
        specs = [scalar] + [near] * (len(operands) - 1)
        scratch = [*buffers, work, passed, trig]
        aliases = {}
        final = not shapes
        if final:
            shapes = [block(*spectrum.shape)]
            scratch += [
                pltpu.VMEM((rows, span, LANES), jnp.float32),
                pltpu.SemaphoreType.DMA((rows,)),
            ]
            if out is not None:
                aliases = {len(operands): 0}
                operands.append(out)
                specs.append(far)
        return pl.pallas_call(
            functools.partial(kernel, chunk, freqs, final),
            in_specs=specs,
            out_specs=[far if final else near] * len(shapes),
            out_shape=shapes,
            scratch_shapes=scratch,
            input_output_aliases=aliases,
            compiler_params=params(24),
            cost_estimate=cost(2 * 40 * span * points, 4 * 4 * span * points),
            name=name,
        )(*operands)

    groups = freqs // TILE

    def two_steps(chunk, state, halo, tables, shapes=(), out=None):
        buffers = [pltpu.VMEM((2, groups, rows + 8, ND, TILE, LANES), jnp.float32)]
        name = "two_substeps"
        return advance(
            two_steps_kernel, name, chunk, state, halo, tables, shapes, buffers, out
        )

    def one_step(chunk, state, halo, tables, shapes=(), out=None):
        buffers = [pltpu.VMEM((groups, rows + 4, ND, TILE, LANES), jnp.float32)]
        name = "one_substep"
        return advance(
            one_step_kernel, name, chunk, state, halo, tables, shapes, buffers, out
        )

    narrow = [tiles(ONE), tiles(ONE), tiles(ND)]
    states = []
    halos = []
    even, odd, rest = source(0)
    states.append((even, odd, rest))
    halos.append(exchange(even, odd))
    even, odd, kit = source(1)
    states.append((even, odd))
    tables = coast(halos[0][1], kit)
    halo = [lax.ppermute(even, BLOCKS, even_swaps), lax.ppermute(odd, BLOCKS, first_swaps)]
    odd, halos[0] = lax.optimization_barrier((odd, halos[0]))
    halos.append((*halo, lax.ppermute(odd, BLOCKS, later_swaps)))
    for chunk in range(CHUNKS):
        if WIDE_FIRST[chunk]:
            made = two_steps(chunk, states[chunk], halos[chunk], tables, narrow)
        else:
            made = one_step(chunk, states[chunk], halos[chunk], tables, [tiles(TWO)] * 2)
        states[chunk] = made
        halos[chunk] = exchange(*made[:2])
    out = None
    for chunk in range(CHUNKS):
        step = one_step if WIDE_FIRST[chunk] else two_steps
        (out,) = step(chunk, states[chunk], halos[chunk], tables, out=out)
    return out


def solution(mesh):
    in_specs = (
        P(None, ("comp", "space")),
        P(None, ("comp", "space")),
        P(),
        P(),
        P(),
        P(),
        P(),
        P(),
        P("space", None),
        P("space", None),
    )
    out_specs = P(None, ("comp", "space"))
    return jax.shard_map(
        per_device, mesh=mesh, in_specs=in_specs, out_specs=out_specs, check_vma=False
    )
```
